32 devices in a mesh: grp: 4 (over z), slab: 8 (over y, x, core).
Axes of the slice: x: 2, y: 2, z: 4, core: 2. Of those that a mesh axis runs over, the one named last changes fastest.
Arguments:
- spectra: bfloat16 [16384, 2048], P(('grp', 'slab')), may hold values from -6 to 6
- ctf_sq: bfloat16 [16384, 1024], P(('grp', 'slab')), may hold values from 0.049804688 to 1
- dest: int32 [16384, 1], P(('grp', 'slab')), may hold values from 0 to 7; in each aligned block of 512 rows (0 to 511, 512 to 1023, ...) at most 128 rows name the same one
- block: int32 [16384], P(('grp', 'slab')), may hold values from 0 to 63
- pattern: int32 [16384], P(('grp', 'slab')), may hold values from 0 to 63
- pattern_table: bfloat16 [64, 8], replicated, may hold values from 0.049804688 to 1
- tau: float32 [1024], replicated, may hold values from 0.5 to 4
Outputs:
- image: float32 [2, 16, 256, 1024], P(None, 'grp', None, 'slab')
The draws below stay inside these ranges and needn't reach their ends.
Inputs may be any that keep to these rules, and one draw needn't show every extreme that they name: `dest`: among the rows of one device at most 128 name the same slab; in some device's rows one slab is named by exactly 128.
All inputs are finite; a program needn't handle non-finite values.
Results may differ from the reference program's by a relative error of at most 0.0003.
Values may be sent and summed in bfloat16 or wider, within the bound.
No kernel may reach another device: no remote copies, remote signals or barrier semaphores. Data moves between devices by JAX's collectives and lax.ppermute only.
A program may use at most 192 MiB of HBM per device.

```python
import math
import jax
import jax.numpy as jnp
import numpy as np
from jax import lax

L = 1024
KZ_DEV = 32
RB = 8
NW = 64
YWIN = 16
ROWS_DEV = 512
CAP = 128
NBLK = 64
NZ = 256
ROWS = 16384
N_SLAB = 8


def with_ends(entries, rng, smallest, high):
    longest = entries.shape.index(max(entries.shape))
    spots = []
    for shift in (0, 1):
        where = [jax.random.randint(jax.random.fold_in(rng, axis), (), 0, length) for axis, length in enumerate(entries.shape)]
        where[longest] = (where[longest] + shift) % entries.shape[longest]
        spots.append(tuple(where))
    return entries.at[spots[0]].set(smallest).at[spots[1]].set(high)


def level_of(key, dims, cuts, least, top_value):
    def one(position, shards_of):
        steps = jax.random.uniform(jax.random.fold_in(jax.random.fold_in(key, 6), position), (shards_of,), jnp.float32, least / len(cuts), top_value / len(cuts))
        return jnp.repeat(jnp.exp(steps), dims[position] // shards_of).reshape((-1,) + (1,) * (len(dims) - position - 1))

    level = one(*cuts[0])
    for cut in cuts[1:]:
        level = level * one(*cut)
    return level


def deal_out(own_key, own, number, rows, number_of, top, most, lean):
    order = jax.random.permutation(own_key, number_of)
    heavy_load, common = portions_of(number_of, rows * top, most, lean, True), portions_of(number_of, rows * top, most, lean, False)
    places = jnp.arange(number_of)

    def named(lengths, turn):
        used = int((lengths > 0).sum())
        fixed = max(1, used // 4)
        shifted = fixed + (places - fixed + turn * (used - fixed)) % max(1, number_of - fixed)
        return jnp.zeros((number_of,), jnp.int32).at[order[jnp.where(places < fixed, places, shifted)]].set(jnp.asarray(lengths, jnp.int32))

    lengths = jnp.where(number % 4 == 0, named(heavy_load, number // 4), named(common, number - number // 4 - 1))
    mixed = jax.random.permutation(jax.random.fold_in(own, 3), number_of)
    donor, receiver = mixed[0:number_of // 2 * 2:2], mixed[1:number_of // 2 * 2:2]
    slack = jnp.minimum(lengths[donor] - 1, most - lengths[receiver]) // 2
    slack = jnp.where((donor == order[0]) | (receiver == order[0]) | (lengths[receiver] == 0), 0, jnp.maximum(slack, 0))
    shifted = jax.random.randint(jax.random.fold_in(own, 4), (number_of // 2,), 0, 1 << 20) % (slack + 1)
    lengths = lengths.at[donor].add(-shifted).at[receiver].add(shifted)
    labels = jnp.searchsorted(jnp.cumsum(lengths), jnp.arange(rows * top), side="right").astype(jnp.int32)
    listing = labels.reshape(top, rows).T
    listing = listing[jax.random.permutation(jax.random.fold_in(own, 1), rows)]
    turn = jax.random.randint(jax.random.fold_in(own, 2), (rows, 1), 0, top)
    return jnp.take_along_axis(listing, (jnp.arange(top)[None, :] + turn) % top, axis=1)


def portions_of(number_of, total, reach, lean, full):
    loads = [(1 << 20) // math.isqrt(rank ** lean) + 1 for rank in range(1, number_of + 1)]
    largest = reach if full else min(reach, max(-(-total // number_of), total * loads[0] // sum(loads)))
    least = 1 if total - largest >= number_of - 1 else 0
    given, rest = [largest] + [least] * (number_of - 1), total - largest - least * (number_of - 1)
    while rest > 0:
        candidates = [i for i in range(1, number_of) if given[i] < largest] or [i for i in range(1, number_of) if given[i] < reach]
        whole, left = sum([loads[i] for i in candidates]), rest
        for i in candidates:
            addition = min(reach - given[i], max(1, left * loads[i] // whole), rest)
            given[i] = given[i] + addition
            rest = rest - addition
    return np.array(given)


def scatter_about(rng, extent, spread, bound, pieces=(), kind=jnp.bfloat16):
    entries = spread * jax.random.normal(rng, extent, jnp.float32)
    if pieces:
        entries = entries * level_of(rng, extent, pieces, -0.22, 0.18)
    return jnp.clip(entries, -bound, bound).astype(kind)


def setup_inputs(seed: int = 0) -> dict:
    seeds = jax.random.split(jax.random.key(seed), 8)
    spectra = scatter_about(seeds[0], (ROWS, 2 * L), 1.0, 6.0, ((0, 32),))
    ctf_sq = jnp.clip(jnp.exp(math.log(1.0) - 2.9996462 * jax.random.uniform(seeds[1], (ROWS, L), jnp.float32) ** level_of(seeds[1], (ROWS, L), ((0, 32),), -0.2, 0.2)), 0.049804688, 1.0).astype(jnp.bfloat16)
    dest_keys = jax.random.split(jax.random.fold_in(seeds[2], 1), ROWS // ROWS_DEV)
    dest_turns = jax.random.permutation(jax.random.fold_in(seeds[2], 3), ROWS // ROWS_DEV)
    dest = jax.vmap(lambda own, number: deal_out(jax.random.fold_in(seeds[2], 2), own, number, ROWS_DEV, N_SLAB, 1, CAP, 2))(dest_keys, dest_turns).reshape((ROWS, 1))
    block = with_ends(jax.random.randint(seeds[3], (ROWS,), 0, NBLK), jax.random.fold_in(seeds[3], 1), 0, NBLK - 1).astype(jnp.int32)
    pattern = with_ends(jax.random.randint(seeds[4], (ROWS,), 0, NW), jax.random.fold_in(seeds[4], 1), 0, NW - 1).astype(jnp.int32)
    pattern_table = jnp.clip(jax.random.uniform(seeds[5], (NW, RB), jnp.float32, 0.049804688, 1.0), 0.049804688, 1.0).astype(jnp.bfloat16)
    tau = jnp.clip(jnp.exp(jax.random.uniform(seeds[6], (L,), jnp.float32, math.log(0.5), math.log(4.0))), 0.5, 4.0)
    return {"spectra": spectra, "ctf_sq": ctf_sq, "dest": dest, "block": block, "pattern": pattern, "pattern_table": pattern_table, "tau": tau}


def reference(spectra, ctf_sq, dest, block, pattern, pattern_table, tau):
    total_rows = spectra.shape[0]
    step_rows = min(1024, total_rows)
    num_steps = total_rows // step_rows
    table_f = pattern_table.astype(jnp.float32)
    global_block = dest[:, 0] * NBLK + block
    volume_rows = N_SLAB * YWIN * KZ_DEV

    def accumulate(volume, index):
        first_row = (index * step_rows).astype(jnp.int32)
        spec_part = lax.dynamic_slice_in_dim(spectra, first_row, step_rows, 0).astype(jnp.float32)
        ctf_part = lax.dynamic_slice_in_dim(ctf_sq, first_row, step_rows, 0).astype(jnp.float32)
        payload = jnp.concatenate([spec_part, ctf_part], axis=1)
        pattern_part = lax.dynamic_slice_in_dim(pattern, first_row, step_rows, 0)
        block_part = lax.dynamic_slice_in_dim(global_block, first_row, step_rows, 0)
        weights = table_f[pattern_part]
        for inner in range(RB):
            volume = volume.at[block_part * RB + inner].add(weights[:, inner:inner + 1] * payload)
        return volume, None

    start_volume = jnp.zeros((volume_rows, 3 * L), jnp.float32)
    volume, unused = lax.scan(accumulate, start_volume, jnp.arange(num_steps, dtype=jnp.int32))
    volume = volume.reshape(N_SLAB, YWIN, KZ_DEV, 3, L)
    filtered = volume[:, :, :, 0:2, :] / (volume[:, :, :, 2:3, :] + tau)
    filtered = jnp.transpose(filtered, (1, 0, 2, 3, 4)).reshape(YWIN, NZ, 2, L)
    complex_field = lax.complex(filtered[:, :, 0, :], filtered[:, :, 1, :])
    transformed = jnp.fft.ifft(complex_field, axis=1, norm="ortho")
    return jnp.stack([jnp.real(transformed), jnp.imag(transformed)]).astype(jnp.float32)
```

```python
import functools
import math

import jax
import jax.numpy as jnp
import numpy as np
from jax import lax
from jax.experimental import pallas as pl
from jax.experimental.pallas import tpu as pltpu
from jax.sharding import PartitionSpec as P

KZ_DEV = 32
YWIN = 16
NBLK = 64
LANES = 128
ALIGN = 16
TOP = 32767.0
STEPS = 256.0
VMEM = 60 * 1024 * 1024

WHOLE = pl.BlockSpec(memory_space=pltpu.VMEM)
SCALARS = pl.BlockSpec(memory_space=pltpu.SMEM)


def params():
    return pltpu.CompilerParams(vmem_limit_bytes=VMEM)


def iota(shape, axis):
    return lax.broadcasted_iota(jnp.int32, shape, axis)


def plan_kernel(slabs, window, dest_ref, block_ref, pattern_ref, table_ref, order_ref, meta_ref):
    rows = dest_ref.shape[1]
    dest = dest_ref[...]
    mine = (dest == iota((slabs, rows), 0)).astype(jnp.float32)
    before = (iota((rows, rows), 0) < iota((rows, rows), 1)).astype(jnp.bfloat16)
    rank = jnp.dot(mine.astype(jnp.bfloat16), before, preferred_element_type=jnp.float32)
    counts = jnp.sum(mine, axis=1, keepdims=True)
    slab_of = iota((slabs, rows), 0)
    first = jnp.sum(jnp.where(slab_of < dest, counts, 0.0), axis=0, keepdims=True)
    target = (first + jnp.sum(mine * rank, axis=0, keepdims=True)).astype(jnp.int32)
    order = (target == iota((rows, rows), 0)).astype(jnp.bfloat16)
    order_ref[...] = order
    ids = (pattern_ref[...] == iota((table_ref.shape[1], rows), 0)).astype(jnp.bfloat16)
    weights = jnp.dot(table_ref[...], ids, preferred_element_type=jnp.float32)
    line = iota((8, rows), 0)
    named = jnp.where(line == 0, dest, jnp.where(line == 1, block_ref[...], 0)).astype(jnp.float32)
    given = jnp.concatenate([weights, named], axis=0).astype(jnp.bfloat16)
    ordered = lax.dot_general(given, order, (((1,), (1,)), ((), ())), preferred_element_type=jnp.float32)
    start = jnp.sum(jnp.where(slab_of < iota((slabs, rows), 1), counts, 0.0), axis=0, keepdims=True)
    start = jnp.minimum(start.astype(jnp.int32) // ALIGN, (rows - window) // ALIGN).astype(jnp.float32)
    ordered = jnp.where(iota((16, rows), 0) == 10, start, ordered)
    meta_ref[...] = ordered.astype(jnp.bfloat16)


def plan_rows(slabs, window, dest, block, pattern, table):
    rows = dest.shape[0]
    return pl.pallas_call(
        functools.partial(plan_kernel, slabs, window),
        out_shape=(
            jax.ShapeDtypeStruct((rows, rows), jnp.bfloat16),
            jax.ShapeDtypeStruct((16, rows), jnp.bfloat16),
        ),
        in_specs=[WHOLE] * 4,
        out_specs=(WHOLE, WHOLE),
        compiler_params=params(),
        name="plan_rows",
    )(dest.reshape(1, rows), block.reshape(1, rows), pattern.reshape(1, rows), table.T)


def sort_kernel(slabs, width, me_ref, order_ref, x_ref, *out_refs):
    order = order_ref[...]
    for offset in range(slabs):
        column = jnp.bitwise_xor(me_ref[0], offset)
        if len(x_ref.shape) == 3:
            piece = x_ref[column]
        else:
            piece = x_ref[:, pl.ds(pl.multiple_of(column * width, width), width)]
        out_refs[offset][...] = jnp.dot(order, piece, preferred_element_type=jnp.float32).astype(jnp.bfloat16)


def sort_columns(slabs, me, order, x, part, kx):
    rows, width = order.shape[0], kx // slabs
    if width % LANES:
        x = lax.slice_in_dim(x, part * kx, (part + 1) * kx, axis=1)
        x = x.reshape(rows, slabs, width).transpose(1, 0, 2)
        x_spec = pl.BlockSpec((slabs, rows, width), lambda i, s: (0, 0, 0))
    else:
        x_spec = pl.BlockSpec((rows, kx), lambda i, s: (0, part))
    return pl.pallas_call(
        functools.partial(sort_kernel, slabs, width),
        out_shape=[jax.ShapeDtypeStruct((rows, width), jnp.bfloat16)] * slabs,
        grid_spec=pltpu.PrefetchScalarGridSpec(
            num_scalar_prefetch=1,
            grid=(1,),
            in_specs=[pl.BlockSpec((rows, rows), lambda i, s: (0, 0)), x_spec],
            out_specs=[pl.BlockSpec((rows, width), lambda i, s: (0, 0))] * slabs,
        ),
        compiler_params=params(),
        name="sort_columns",
    )(me, order, x)


def exchange(pieces):
    slabs = len(pieces)
    return [pieces[0]] + [
        lax.ppermute(pieces[o], "slab", [(i, i ^ o) for i in range(slabs)]) for o in range(1, slabs)
    ]


def spread_kernel(slabs, window, me_ref, meta_ref, weight_ref, start_ref, all_ref, here_ref, line_ref, scalar_ref, sem):
    slab = pl.program_id(0)
    rows = meta_ref.shape[2]

    @pl.when(slab == 0)
    def _():
        pick = (iota((16, LANES), 0) == iota((16, LANES), 1)).astype(jnp.bfloat16)
        for offset in range(slabs):
            meta = meta_ref[jnp.bitwise_xor(me_ref[0], offset)]
            all_ref[offset] = lax.dot_general(
                meta, pick, (((0,), (0,)), ((), ())), preferred_element_type=jnp.float32
            ).astype(jnp.bfloat16)
            line_ref[offset : offset + 1, :] = meta.astype(jnp.float32)[10:11, 0:LANES].astype(jnp.int32) * ALIGN
        copy = pltpu.make_async_copy(line_ref, scalar_ref, sem)
        copy.start()
        copy.wait()
        start_ref[...] = line_ref[...]

    for offset in range(slabs):
        start = pl.multiple_of(scalar_ref[offset, slab], ALIGN)
        here_ref[offset * window : (offset + 1) * window, :] = all_ref[offset, pl.ds(start, window), :]
    pick = (iota((16, LANES), 0) == iota((16, LANES), 1)).astype(jnp.bfloat16)
    meta = lax.dot_general(pick, here_ref[...], (((1,), (1,)), ((), ())), preferred_element_type=jnp.float32)
    weights = meta[0:8]
    total = weights.shape[1]
    block = jnp.where(meta[8:9] == slab.astype(jnp.float32), meta[9:10], -1.0)
    block = jnp.broadcast_to(block, (8, total))
    for b in range(0, NBLK, 2):
        pair = [jnp.where(block == float(b + i), weights, 0.0) for i in range(2)]
        weight_ref[0, b * 8 : b * 8 + 16, :] = jnp.concatenate(pair, axis=0).astype(jnp.bfloat16)


def spread_weights(window, me, meta):
    slabs, _, rows = meta.shape
    total = slabs * window
    return pl.pallas_call(
        functools.partial(spread_kernel, slabs, window),
        out_shape=(
            jax.ShapeDtypeStruct((slabs, NBLK * 8, total), jnp.bfloat16),
            jax.ShapeDtypeStruct((slabs, LANES), jnp.int32),
        ),
        grid_spec=pltpu.PrefetchScalarGridSpec(
            num_scalar_prefetch=1,
            grid=(slabs,),
            in_specs=[pl.BlockSpec((slabs, 16, rows), lambda d, s: (0, 0, 0))],
            out_specs=(
                pl.BlockSpec((1, NBLK * 8, total), lambda d, s: (d, 0, 0)),
                pl.BlockSpec((slabs, LANES), lambda d, s: (0, 0)),
            ),
            scratch_shapes=[
                pltpu.VMEM((slabs, rows, LANES), jnp.bfloat16),
                pltpu.VMEM((total, LANES), jnp.bfloat16),
                pltpu.VMEM((slabs, LANES), jnp.int32),
                pltpu.SMEM((slabs, LANES), jnp.int32),
                pltpu.SemaphoreType.DMA,
            ],
        ),
        compiler_params=params(),
        name="spread_weights",
    )(me, meta)


def volume_kernel(slabs, window, start_ref, weight_ref, *refs):
    piece_refs, out_ref, here_ref = refs[:slabs], refs[slabs], refs[slabs + 1]
    slab = pl.program_id(0)
    for offset in range(slabs):
        start = pl.multiple_of(start_ref[offset, slab], ALIGN)
        here_ref[offset * window : (offset + 1) * window, :] = piece_refs[offset][pl.ds(start, window), :]
    sums = jnp.dot(weight_ref[0], here_ref[...], preferred_element_type=jnp.float32)
    out_ref[:, 0] = sums.reshape(YWIN, KZ_DEV, sums.shape[1])


def volume_sums(window, starts, weights, pieces):
    slabs = len(pieces)
    rows, width = pieces[0].shape
    total = slabs * window
    return pl.pallas_call(
        functools.partial(volume_kernel, slabs, window),
        out_shape=jax.ShapeDtypeStruct((YWIN, slabs, KZ_DEV, width), jnp.float32),
        grid_spec=pltpu.PrefetchScalarGridSpec(
            num_scalar_prefetch=1,
            grid=(slabs,),
            in_specs=[pl.BlockSpec((1, NBLK * 8, total), lambda d, s: (d, 0, 0))]
            + [pl.BlockSpec((rows, width), lambda d, s: (0, 0))] * slabs,
            out_specs=pl.BlockSpec((YWIN, 1, KZ_DEV, width), lambda d, s: (0, d, 0, 0)),
            scratch_shapes=[pltpu.VMEM((total, width), jnp.bfloat16)],
        ),
        compiler_params=params(),
        name="volume_sums",
    )(starts, weights, *pieces)


def encode(x):
    rows, width = x.shape
    groups = rows // 8
    tiles = x.reshape(groups, 8, width)
    size = jnp.abs(tiles)
    most = jnp.max(jnp.max(size, axis=1), axis=1, keepdims=True)
    level = jnp.ceil(jnp.log2(jnp.maximum(most, 1e-30)) * STEPS) + 1.0
    inverse = jnp.broadcast_to(jnp.exp2(level * (-1.0 / STEPS)), (groups, width)).reshape(groups, 1, width)
    share = jnp.maximum(size * inverse, 1e-12)
    root = jnp.minimum(share * lax.rsqrt(share) * TOP + 0.5, TOP)
    code = jnp.where(tiles < 0, -root, root).reshape(rows, width).astype(jnp.int32).astype(jnp.int16)
    eye = iota((width, width), 0) == iota((width, width), 1)
    lines = [
        jnp.sum(jnp.where(eye, level[i * width : (i + 1) * width], 0.0), axis=0, keepdims=True)
        for i in range(groups // width)
    ]
    lines.append(jnp.zeros((ALIGN - len(lines), width), jnp.float32))
    return code, jnp.concatenate(lines, axis=0).astype(jnp.int32).astype(jnp.int16)


def decode(code, lines):
    rows, width = code.shape
    groups = rows // 8
    x = code.astype(jnp.int32).astype(jnp.float32)
    lines = lines.astype(jnp.int32).astype(jnp.float32)
    eye = iota((width, width), 0) == iota((width, width), 1)
    level = jnp.concatenate(
        [jnp.sum(jnp.where(eye, lines[i : i + 1], 0.0), axis=1, keepdims=True) for i in range(groups // width)],
        axis=0,
    )
    scale = jnp.exp2(level * (1.0 / STEPS)) * (1.0 / (TOP * TOP))
    scale = jnp.broadcast_to(scale, (groups, width)).reshape(groups, 1, width)
    return ((x * jnp.abs(x)).reshape(groups, 8, width) * scale).reshape(rows, width)


def hop_kernel(has_prev, idx_ref, sums_ref, *refs):
    out_ref = refs[-1]
    rows = sums_ref.shape[1]
    x = sums_ref[0]
    if has_prev:
        x = x + decode(refs[0][0, :rows, :], refs[0][0, rows:, :])
    code, lines = encode(x)
    out_ref[0, :rows, :] = code
    out_ref[0, rows:, :] = lines


def hop(index, sums, count, prev, place):
    _, rows, width = sums.shape
    shape = (1, rows + ALIGN, width)
    in_specs = [pl.BlockSpec((1, rows, width), lambda i, s: (s[i], 0, 0))]
    operands = [sums]
    if prev is not None:
        in_specs.append(pl.BlockSpec(shape, lambda i, s: (place(i), 0, 0)))
        operands.append(prev)
    return pl.pallas_call(
        functools.partial(hop_kernel, prev is not None),
        out_shape=jax.ShapeDtypeStruct((count, rows + ALIGN, width), jnp.int16),
        grid_spec=pltpu.PrefetchScalarGridSpec(
            num_scalar_prefetch=1,
            grid=(count,),
            in_specs=in_specs,
            out_specs=pl.BlockSpec(shape, lambda i, s: (i, 0, 0)),
        ),
        compiler_params=params(),
        name="hop",
    )(index, *operands)


def along_z(sums, z, groups):
    half = groups // 2
    far = z >= half

    def portions(first, count):
        r = jnp.arange(first, first + count, dtype=jnp.int32)
        return jnp.where(far, groups - 1 - r, r)

    def both(pairs):
        return pairs + [(groups - 1 - a, groups - 1 - b) for a, b in pairs]

    ends = []
    prev = None
    for k in range(1, half):
        payload = hop(portions(k, groups - k), sums, groups - k, prev, lambda i: i + 1)
        prev = lax.ppermute(payload, "grp", both([(k - 1, k)]))
        ends.append((prev, 0))
    payload = hop(portions(half, half), sums, half, prev, lambda i: i + 1)
    prev = lax.ppermute(payload, "grp", both([(half - 1, half)]))
    ends.append((prev, 0))
    place = lambda i: half - 1 - i
    for j in range(half - 1, 0, -1):
        payload = hop(portions(0, j), sums, j, prev, place)
        prev = lax.ppermute(payload, "grp", both([(j, j - 1)]))
        ends.append((prev, j - 1))
        place = lambda i: i
    return ends


def image_kernel(parts, zs, own_ref, *refs):
    tau_ref, high_ref, low_ref, out_ref = refs[-4:]
    each = len(refs[:-4]) // 3
    volume = []
    for c in range(3):
        sums_ref, coded = refs[c * each], refs[c * each + 1 : (c + 1) * each]
        rows = sums_ref.shape[1]
        x = sums_ref[0]
        for ref in coded:
            x = x + decode(ref[0, :rows, :], ref[0, rows:, :])
        volume.append(x)
    below = volume[2] + tau_ref[...]
    columns = []
    for c in range(2):
        x = volume[c] / below
        columns += [x[k * zs : (k + 1) * zs] for k in range(parts)]
    x = jnp.concatenate(columns, axis=1)
    x_high = x.astype(jnp.bfloat16)
    x_low = (x - x_high.astype(jnp.float32)).astype(jnp.bfloat16)
    dot = functools.partial(jnp.dot, preferred_element_type=jnp.float32)
    y = dot(high_ref[...], x_high) + (dot(high_ref[...], x_low) + dot(low_ref[...], x_high))
    span = x.shape[1] // 2
    width = span // parts
    real = y[:zs, :span] - y[zs:, span:]
    imag = y[zs:, :span] + y[:zs, span:]
    for k in range(parts):
        out_ref[0, k] = real[:, k * width : (k + 1) * width]
        out_ref[1, k] = imag[:, k * width : (k + 1) * width]


def image_of(own, fields, tau, zs):
    rows, width = fields[0][0].shape[1:]
    parts = rows // zs
    operands, specs = [], []
    for sums, ends in fields:
        operands.append(sums)
        specs.append(pl.BlockSpec((1, rows, width), lambda i, s: (s[0], 0, 0)))
        for payload, place in ends:
            operands.append(payload)
            specs.append(pl.BlockSpec((1, rows + ALIGN, width), functools.partial(lambda place, i, s: (place, 0, 0), place)))
    steps = np.arange(zs)
    angles = (steps[:, None] * steps[None, :] % zs) * (2.0 * math.pi / zs)
    table = (np.concatenate([np.cos(angles), np.sin(angles)], axis=0) / math.sqrt(zs)).astype(np.float32)
    high = table.astype(jnp.bfloat16)
    low = (table - high.astype(np.float32)).astype(jnp.bfloat16)
    for x in (tau.reshape(1, width), jnp.asarray(high), jnp.asarray(low)):
        operands.append(x)
        specs.append(pl.BlockSpec(x.shape, lambda i, s: (0, 0)))
    return pl.pallas_call(
        functools.partial(image_kernel, parts, zs),
        out_shape=jax.ShapeDtypeStruct((2, parts, zs, width), jnp.float32),
        grid_spec=pltpu.PrefetchScalarGridSpec(
            num_scalar_prefetch=1,
            grid=(1,),
            in_specs=specs,
            out_specs=pl.BlockSpec((2, parts, zs, width), lambda i, s: (0, 0, 0, 0)),
        ),
        compiler_params=params(),
        name="image_of",
    )(own, *operands)


def on_device(spectra, ctf_sq, dest, block, pattern, pattern_table, tau):
    slabs, groups = lax.axis_size("slab"), lax.axis_size("grp")
    rows, kx = ctf_sq.shape
    capacity = max(2, 2 * rows // slabs)
    window = min(rows, -(-capacity // ALIGN) * ALIGN + ALIGN)
    width = kx // slabs
    slab, z = lax.axis_index("slab"), lax.axis_index("grp")
    me = slab.astype(jnp.int32).reshape(1)
    order, meta = plan_rows(slabs, window, dest, block, pattern, pattern_table)
    meta = lax.all_gather(meta, "slab")
    sources = ((ctf_sq, 0), (spectra, 0), (spectra, 1))
    pieces = [exchange(sort_columns(slabs, me, order, x, part, kx)) for x, part in sources]
    weights, starts = spread_weights(window, me, meta)
    fields = []
    for piece in pieces:
        sums = volume_sums(window, starts, weights, piece)
        sums = sums.reshape(groups, YWIN // groups * slabs * KZ_DEV, width)
        fields.append((sums, along_z(sums, z, groups)))
    tau_here = lax.dynamic_slice_in_dim(tau, slab * width, width, 0)
    own = z.astype(jnp.int32).reshape(1)
    return image_of(own, [fields[1], fields[2], fields[0]], tau_here, KZ_DEV * slabs)


def solution(mesh):
    in_specs = (
        P(("grp", "slab"), None),
        P(("grp", "slab"), None),
        P(("grp", "slab"), None),
        P(("grp", "slab")),
        P(("grp", "slab")),
        P(),
        P(),
    )
    out_specs = P(None, "grp", None, "slab")
    return jax.shard_map(
        on_device, mesh=mesh, in_specs=in_specs, out_specs=out_specs, check_vma=False
    )
```

```python
import functools
import math

import jax
import jax.numpy as jnp
import numpy as np
from jax import lax
from jax.experimental import pallas as pl
from jax.experimental.pallas import tpu as pltpu
from jax.sharding import PartitionSpec as P

KZ_DEV = 32
YWIN = 16
NBLK = 64
LANES = 128
ALIGN = 16
TIE = 1
TOP = 32767.0
STEPS = 256.0
VMEM = 60 * 1024 * 1024

WHOLE = pl.BlockSpec(memory_space=pltpu.VMEM)
SCALARS = pl.BlockSpec(memory_space=pltpu.SMEM)


def params(width):
    return pltpu.CompilerParams(vmem_limit_bytes=VMEM if width < LANES else VMEM // 2)


def near(x):
    return pltpu.with_memory_space_constraint(x, pltpu.VMEM)


def far(x):
    return pltpu.with_memory_space_constraint(x, pltpu.HBM)


def cost(micros):
    return pl.CostEstimate(flops=0, bytes_accessed=int(micros * 3.0e6), transcendentals=0)


def iota(shape, axis):
    return lax.broadcasted_iota(jnp.int32, shape, axis)


def plan(slabs, window, dest, block, pattern, table):
    rows = dest.shape[1]
    mine = (dest == iota((slabs, rows), 0)).astype(jnp.float32)
    before = (iota((rows, rows), 0) < iota((rows, rows), 1)).astype(jnp.bfloat16)
    rank = jnp.dot(mine.astype(jnp.bfloat16), before, preferred_element_type=jnp.float32)
    counts = jnp.sum(mine, axis=1, keepdims=True)
    slab_of = iota((slabs, rows), 0)
    first = jnp.sum(jnp.where(slab_of < dest, counts, 0.0), axis=0, keepdims=True)
    target = (first + jnp.sum(mine * rank, axis=0, keepdims=True)).astype(jnp.int32)
    order = (target == iota((rows, rows), 0)).astype(jnp.bfloat16)
    ids = (pattern == iota((table.shape[1], rows), 0)).astype(jnp.bfloat16)
    weights = jnp.dot(table, ids, preferred_element_type=jnp.float32)
    line = iota((8, rows), 0)
    named = jnp.where(line == 0, dest, jnp.where(line == 1, block, 0)).astype(jnp.float32)
    given = jnp.concatenate([weights, named], axis=0).astype(jnp.bfloat16)
    ordered = lax.dot_general(given, order, (((1,), (1,)), ((), ())), preferred_element_type=jnp.float32)
    start = jnp.sum(jnp.where(slab_of < iota((slabs, rows), 1), counts, 0.0), axis=0, keepdims=True)
    start = jnp.minimum(start.astype(jnp.int32) // ALIGN, (rows - window) // ALIGN).astype(jnp.float32)
    meta = jnp.where(iota((16, rows), 0) == 10, start, ordered).astype(jnp.bfloat16)
    return order, meta


def piece_of(x_ref, column, width):
    if len(x_ref.shape) == 3:
        return x_ref[column]
    return x_ref[:, pl.ds(pl.multiple_of(column * width, width), width)]


def by_slab(x, slabs, width):
    if width % LANES == 0:
        return x
    return x.reshape(x.shape[0], -1, width).transpose(1, 0, 2)


def sorted_piece(order, x_ref, column, width):
    piece = piece_of(x_ref, column, width)
    return jnp.dot(order, piece, preferred_element_type=jnp.float32).astype(jnp.bfloat16)


def plan_kernel(slabs, window, width, me_ref, *refs):
    ids_refs, table_ref, x_refs, order_ref, out_refs = refs[0:2], refs[2], refs[3:5], refs[5], refs[6:]
    rows = order_ref.shape[1]
    lines = 16 * (rows // width)
    for half in range(2):
        ids = ids_refs[half][...]
        order, meta = plan(slabs, window, ids[0:1], ids[1:2], ids[2:3], table_ref[...])
        order_ref[half] = order
        for i, out in enumerate(out_refs):
            column = jnp.bitwise_xor(me_ref[0], 2 * i)
            out[half * rows : (half + 1) * rows, :] = sorted_piece(order, x_refs[half], column, width)
            for j in range(rows // width):
                at = 2 * rows + half * lines + 16 * j
                out[at : at + 16, :] = meta[:, j * width : (j + 1) * width]


def plan_rows(slabs, window, me, ids, table, xs):
    rows, kx = xs[0].shape
    width = kx // slabs
    out = jax.ShapeDtypeStruct((2 * rows + 32 * (rows // width), width), jnp.bfloat16)
    done = pl.pallas_call(
        functools.partial(plan_kernel, slabs, window, width),
        out_shape=[jax.ShapeDtypeStruct((2, rows, rows), jnp.bfloat16)] + [out] * (slabs // 2),
        in_specs=[SCALARS] + [WHOLE] * 5,
        out_specs=[WHOLE] * (1 + slabs // 2),
        compiler_params=params(width),
        cost_estimate=cost(6.0),
        name="plan_rows",
    )(me, *[far(x) for x in ids], far(table.T), *[far(by_slab(x, slabs, width)) for x in xs])
    return done[0], done[1:]


def sort_kernel(slabs, width, me_ref, order_ref, *refs):
    x_refs, out_refs = refs[0:2], refs[2:]
    rows = order_ref.shape[1]
    for part in range(2):
        for half in range(2):
            order = order_ref[half]
            for i in range(slabs // 2):
                column = jnp.bitwise_xor(me_ref[0], 2 * i) + part * slabs
                out = out_refs[part * (slabs // 2) + i]
                out[half * rows : (half + 1) * rows, :] = sorted_piece(order, x_refs[half], column, width)


def sort_columns(slabs, me, order, xs):
    rows, width = order.shape[1], xs[0].shape[1] // (2 * slabs)
    done = pl.pallas_call(
        functools.partial(sort_kernel, slabs, width),
        out_shape=[jax.ShapeDtypeStruct((2 * rows, width), jnp.bfloat16)] * slabs,
        in_specs=[SCALARS] + [WHOLE] * 3,
        out_specs=[WHOLE] * slabs,
        compiler_params=params(width),
        cost_estimate=cost(5.0),
        name="sort_columns",
    )(me, order, *[by_slab(x, slabs, width) for x in xs])
    return done[: slabs // 2], done[slabs // 2 :]


def swap(x, slabs, offset):
    return lax.ppermute(x, "slab", [(i, i ^ offset) for i in range(slabs)])


def exchange(pieces, after=None):
    got = [pieces[0]]
    for i in range(1, len(pieces)):
        piece = pieces[i]
        if after is not None:
            piece, after[i] = lax.optimization_barrier((piece, after[i]))
        got.append(swap(piece, 2 * len(pieces), 2 * i))
    return got


def volume_kernel(slabs, window, count, first, idx_ref, *refs):
    piece_refs, refs = refs[: slabs // 2], refs[slabs // 2 :]
    if first:
        sums_ref, code_ref, meta_ref, all_ref, line_ref, scalar_ref, sem = refs
    else:
        meta_ref, sums_ref, code_ref, all_ref, line_ref, scalar_ref, sem = refs
    width = sums_ref.shape[3]
    rows = all_ref.shape[1]
    pick = (iota((16, LANES), 0) == iota((16, LANES), 1)).astype(jnp.bfloat16)
    for offset in range(slabs):
        if first:
            for i in range(rows // width):
                at = 2 * rows + 16 * (offset % 2 * (rows // width) + i)
                meta_ref[offset, :, i * width : (i + 1) * width] = piece_refs[offset // 2][at : at + 16, :]
        meta = meta_ref[offset]
        all_ref[offset] = lax.dot_general(
            meta, pick, (((0,), (0,)), ((), ())), preferred_element_type=jnp.float32
        ).astype(jnp.bfloat16)
        line_ref[offset : offset + 1, :] = meta.astype(jnp.float32)[10:11, 0:LANES].astype(jnp.int32) * ALIGN
    copy = pltpu.make_async_copy(line_ref, scalar_ref, sem)
    copy.start()
    copy.wait()

    def slab_sums(slab):
        about, here = [], []
        for offset in range(slabs):
            start = pl.multiple_of(scalar_ref[offset, slab], ALIGN)
            about.append(all_ref[offset, pl.ds(start, window), :])
            start = pl.multiple_of(offset % 2 * rows + start, ALIGN)
            here.append(piece_refs[offset // 2][pl.ds(start, window), :])
        about, here = jnp.concatenate(about, axis=0), jnp.concatenate(here, axis=0)
        meta = lax.dot_general(pick, about, (((1,), (1,)), ((), ())), preferred_element_type=jnp.float32)
        weights = meta[0:8]
        own = meta[8:9] == jnp.asarray(slab, jnp.float32)
        block = jnp.broadcast_to(jnp.where(own, meta[9:10], -1.0), weights.shape)
        spread = jnp.concatenate([jnp.where(block == float(b), weights, 0.0) for b in range(NBLK)], axis=0)
        sums = jnp.dot(spread.astype(jnp.bfloat16), here, preferred_element_type=jnp.float32)
        sums_ref[:, slab] = sums.reshape(YWIN, KZ_DEV, width)

    if slabs <= 8:
        for slab in range(slabs):
            slab_sums(slab)
    else:
        lax.fori_loop(0, slabs, lambda slab, carry: (slab_sums(slab), carry)[1], 0)
    portion = code_ref.shape[1] - ALIGN
    lines = portion // (slabs * KZ_DEV)
    for i in range(count):
        x = sums_ref[pl.ds(idx_ref[i] * lines, lines)].reshape(portion, width)
        code_ref[i, :portion, :], code_ref[i, portion:, :] = encode(x)


def volume_sums(window, index, count, groups, pieces, meta=None):
    slabs = 2 * len(pieces)
    width = pieces[0].shape[1]
    first = meta is None
    rows = pieces[0].shape[0] // 2
    if first:
        rows = rows * width // (width + 16)
    portion = YWIN // groups * slabs * KZ_DEV
    out_shape = [
        jax.ShapeDtypeStruct((YWIN, slabs, KZ_DEV, width), jnp.float32),
        jax.ShapeDtypeStruct((count, portion + ALIGN, width), jnp.int16),
    ]
    if first:
        out_shape.append(jax.ShapeDtypeStruct((slabs, 16, rows), jnp.bfloat16))
    done = pl.pallas_call(
        functools.partial(volume_kernel, slabs, window, count, first),
        out_shape=out_shape,
        in_specs=[SCALARS] + [WHOLE] * (slabs // 2 + (0 if first else 1)),
        out_specs=[WHOLE] * len(out_shape),
        scratch_shapes=[
            pltpu.VMEM((slabs, rows, LANES), jnp.bfloat16),
            pltpu.VMEM((slabs, LANES), jnp.int32),
            pltpu.SMEM((slabs, LANES), jnp.int32),
            pltpu.SemaphoreType.DMA,
        ],
        compiler_params=params(width),
        cost_estimate=cost(7.0),
        name="volume_sums",
    )(index, *[far(x) for x in pieces], *([] if first else [far(meta)]))
    return done[0].reshape(groups, portion, width), done[1], done[2] if first else meta


def encode(x):
    rows, width = x.shape
    groups = rows // 8
    tiles = x.reshape(groups, 8, width)
    size = jnp.abs(tiles)
    most = jnp.max(jnp.max(size, axis=1), axis=1, keepdims=True)
    level = jnp.ceil(jnp.log2(jnp.maximum(most, 1e-30)) * STEPS) + 1.0
    inverse = jnp.broadcast_to(jnp.exp2(level * (-1.0 / STEPS)), (groups, width)).reshape(groups, 1, width)
    share = jnp.maximum(size * inverse, 1e-12)
    root = jnp.minimum(share * lax.rsqrt(share) * TOP + 0.5, TOP)
    code = jnp.where(tiles < 0, -root, root).reshape(rows, width).astype(jnp.int32).astype(jnp.int16)
    eye = iota((width, width), 0) == iota((width, width), 1)
    lines = [
        jnp.sum(jnp.where(eye, level[i * width : (i + 1) * width], 0.0), axis=0, keepdims=True)
        for i in range(groups // width)
    ]
    lines.append(jnp.zeros((ALIGN - len(lines), width), jnp.float32))
    return code, jnp.concatenate(lines, axis=0).astype(jnp.int32).astype(jnp.int16)


def decode(code, lines):
    rows, width = code.shape
    groups = rows // 8
    x = code.astype(jnp.int32).astype(jnp.float32)
    lines = lines.astype(jnp.int32).astype(jnp.float32)
    eye = iota((width, width), 0) == iota((width, width), 1)
    level = jnp.concatenate(
        [jnp.sum(jnp.where(eye, lines[i : i + 1], 0.0), axis=1, keepdims=True) for i in range(groups // width)],
        axis=0,
    )
    scale = jnp.exp2(level * (1.0 / STEPS)) * (1.0 / (TOP * TOP))
    scale = jnp.broadcast_to(scale, (groups, width)).reshape(groups, 1, width)
    return ((x * jnp.abs(x)).reshape(groups, 8, width) * scale).reshape(rows, width)


def hop_kernel(places, idx_ref, sums_ref, prev_ref, out_ref):
    rows = sums_ref.shape[1]
    for i, place in enumerate(places):
        x = sums_ref[idx_ref[i]] + decode(prev_ref[place, :rows, :], prev_ref[place, rows:, :])
        out_ref[i, :rows, :], out_ref[i, rows:, :] = encode(x)


def hop(index, sums, prev, places):
    _, rows, width = sums.shape
    count = len(places)
    return pl.pallas_call(
        functools.partial(hop_kernel, places),
        out_shape=jax.ShapeDtypeStruct((count, rows + ALIGN, width), jnp.int16),
        in_specs=[SCALARS, WHOLE, WHOLE],
        out_specs=WHOLE,
        compiler_params=params(width),
        cost_estimate=cost(2.0 + count),
        name="hop",
    )(index, far(sums), far(prev))


def portions(z, groups, r):
    return jnp.where(z >= groups // 2, groups - 1 - r, r).astype(jnp.int32)


def along_z(sums, payload, z, groups):
    half = groups // 2
    depth = jnp.minimum(z, groups - 1 - z)
    steps = np.arange(groups)

    def send(payload, pairs):
        return lax.ppermute(payload, "grp", pairs + [(groups - 1 - a, groups - 1 - b) for a, b in pairs])

    def add(r, prev, places):
        return hop(portions(z, groups, r), sums, prev, list(places))

    prev = send(payload, [(0, 1)])
    inward = [None, prev]
    for k in range(2, half):
        prev = send(add(steps[k + 1 :], prev, range(1, groups - k)), [(k - 1, k)])
        inward.append(prev)
    prev = send(add(steps[half:], prev, range(half)), [(half - 1, half)])
    ends = [(prev, 0)]
    places = list(range(half - 1, -1, -1))
    for j in range(half - 1, 1, -1):
        ends.append((send(add(steps[j : j + 1], inward[j - 1], [0]), [(j - 1, j)]), 0))
        prev = send(add(steps[:j], prev, places[:j]), [(j, j - 1)])
        ends.append((prev, j - 1))
        places = list(range(half))
    prev = send(add(jnp.where(depth == 0, 1, steps[:1]), prev, places[:1]), [(1, 0), (0, 1)])
    ends.append((prev, 0))
    return ends


def image_kernel(parts, zs, own_ref, *refs):
    tau_ref, high_ref, low_ref, out_ref = refs[-4:]
    each = len(refs[:-4]) // 3
    volume = []
    for c in range(3):
        sums_ref, coded = refs[c * each], refs[c * each + 1 : (c + 1) * each]
        rows = sums_ref.shape[1]
        x = sums_ref[0]
        for ref in coded:
            x = x + decode(ref[0, :rows, :], ref[0, rows:, :])
        volume.append(x)
    below = volume[2] + tau_ref[...]
    columns = []
    for c in range(2):
        x = volume[c] / below
        columns += [x[k * zs : (k + 1) * zs] for k in range(parts)]
    x = jnp.concatenate(columns, axis=1)
    x_high = x.astype(jnp.bfloat16)
    x_low = (x - x_high.astype(jnp.float32)).astype(jnp.bfloat16)
    dot = functools.partial(jnp.dot, preferred_element_type=jnp.float32)
    y = dot(high_ref[...], x_high) + (dot(high_ref[...], x_low) + dot(low_ref[...], x_high))
    span = x.shape[1] // 2
    width = span // parts
    real = y[:zs, :span] - y[zs:, span:]
    imag = y[zs:, :span] + y[:zs, span:]
    for k in range(parts):
        out_ref[0, k] = real[:, k * width : (k + 1) * width]
        out_ref[1, k] = imag[:, k * width : (k + 1) * width]


def image_of(own, fields, tau, zs):
    rows, width = fields[0][0].shape[1:]
    parts = rows // zs
    operands, specs = [], []
    for sums, ends in fields:
        operands.append(sums)
        specs.append(pl.BlockSpec((1, rows, width), lambda i, s: (s[0], 0, 0)))
        for payload, place in ends:
            operands.append(payload)
            specs.append(pl.BlockSpec((1, rows + ALIGN, width), functools.partial(lambda place, i, s: (place, 0, 0), place)))
    steps = np.arange(zs)
    angles = (steps[:, None] * steps[None, :] % zs) * (2.0 * math.pi / zs)
    table = (np.concatenate([np.cos(angles), np.sin(angles)], axis=0) / math.sqrt(zs)).astype(np.float32)
    high = table.astype(jnp.bfloat16)
    low = (table - high.astype(np.float32)).astype(jnp.bfloat16)
    for x in (tau.reshape(1, width), jnp.asarray(high), jnp.asarray(low)):
        operands.append(x)
        specs.append(pl.BlockSpec(x.shape, lambda i, s: (0, 0)))
    return pl.pallas_call(
        functools.partial(image_kernel, parts, zs),
        out_shape=jax.ShapeDtypeStruct((2, parts, zs, width), jnp.float32),
        grid_spec=pltpu.PrefetchScalarGridSpec(
            num_scalar_prefetch=1,
            grid=(1,),
            in_specs=specs,
            out_specs=pl.BlockSpec((2, parts, zs, width), lambda i, s: (0, 0, 0, 0)),
        ),
        compiler_params=params(width),
        cost_estimate=cost(6.0),
        name="image_of",
    )(own, *[far(x) for x in operands])


def on_device(spectra, ctf_sq, dest, block, pattern, pattern_table, tau):
    slabs, groups = lax.axis_size("slab"), lax.axis_size("grp")
    rows, kx = ctf_sq.shape
    capacity = max(2, 2 * rows // slabs)
    window = min(rows, -(-capacity // ALIGN) * ALIGN + ALIGN)
    width = kx // slabs
    slab, z = lax.axis_index("slab"), lax.axis_index("grp")
    me = slab.astype(jnp.int32).reshape(1)
    ids = jnp.stack([dest[:, 0], block, pattern])
    ids, ctf_sq, spectra = [(x, swap(x, slabs, 1)) for x in (ids, ctf_sq, spectra)]
    order, ctf = plan_rows(slabs, window, me, ids, pattern_table, ctf_sq)
    real, imag = sort_columns(slabs, me, order, spectra)
    pieces = [exchange(ctf)]
    pieces.append(exchange(real, pieces[0]))
    index = portions(z, groups, np.arange(2, groups))
    fields, meta = [], None
    for piece in range(3):
        if piece == 2:
            pieces.append(exchange(imag, [lax.optimization_barrier((x, fields[0][1][0][0]))[0] for x in pieces[1]] if TIE == 1 else [payload0] * len(imag)))
        piece = pieces[piece]
        sums, payload, meta = volume_sums(window, index, groups - 2, groups, piece, meta)
        if not fields:
            payload0 = payload
        fields.append((sums, along_z(sums, payload, z, groups)))
    tau_here = lax.dynamic_slice_in_dim(tau, slab * width, width, 0)
    own = z.astype(jnp.int32).reshape(1)
    return image_of(own, [fields[1], fields[2], fields[0]], tau_here, KZ_DEV * slabs)


def solution(mesh):
    in_specs = (
        P(("grp", "slab"), None),
        P(("grp", "slab"), None),
        P(("grp", "slab"), None),
        P(("grp", "slab")),
        P(("grp", "slab")),
        P(),
        P(),
    )
    out_specs = P(None, "grp", None, "slab")
    return jax.shard_map(
        on_device, mesh=mesh, in_specs=in_specs, out_specs=out_specs, check_vma=False
    )
```

```python
import functools
import math

import jax
import jax.numpy as jnp
import numpy as np
from jax import lax
from jax.experimental import pallas as pl
from jax.experimental.pallas import tpu as pltpu
from jax.sharding import PartitionSpec as P

KZ_DEV = 32
YWIN = 16
NBLK = 64
LANES = 128
ALIGN = 16
TOP = 32767.0
STEPS = 256.0
VMEM = 60 * 1024 * 1024

WHOLE = pl.BlockSpec(memory_space=pltpu.VMEM)
SCALARS = pl.BlockSpec(memory_space=pltpu.SMEM)
UNREAD = pl.BlockSpec(memory_space=pl.ANY)


def params(width):
    return pltpu.CompilerParams(vmem_limit_bytes=VMEM if width < LANES else VMEM // 2)


def far(x):
    return pltpu.with_memory_space_constraint(x, pltpu.HBM)


def cost(micros):
    return pl.CostEstimate(flops=0, bytes_accessed=int(micros * 3.0e6), transcendentals=0)


def iota(shape, axis):
    return lax.broadcasted_iota(jnp.int32, shape, axis)


def plan(slabs, window, dest, block, pattern, table):
    rows = dest.shape[1]
    mine = (dest == iota((slabs, rows), 0)).astype(jnp.float32)
    before = (iota((rows, rows), 0) < iota((rows, rows), 1)).astype(jnp.bfloat16)
    rank = jnp.dot(mine.astype(jnp.bfloat16), before, preferred_element_type=jnp.float32)
    counts = jnp.sum(mine, axis=1, keepdims=True)
    slab_of = iota((slabs, rows), 0)
    first = jnp.sum(jnp.where(slab_of < dest, counts, 0.0), axis=0, keepdims=True)
    target = (first + jnp.sum(mine * rank, axis=0, keepdims=True)).astype(jnp.int32)
    order = (target == iota((rows, rows), 0)).astype(jnp.bfloat16)
    ids = (pattern == iota((table.shape[1], rows), 0)).astype(jnp.bfloat16)
    weights = jnp.dot(table, ids, preferred_element_type=jnp.float32)
    line = iota((8, rows), 0)
    named = jnp.where(line == 0, dest, jnp.where(line == 1, block, 0)).astype(jnp.float32)
    given = jnp.concatenate([weights, named], axis=0).astype(jnp.bfloat16)
    ordered = lax.dot_general(given, order, (((1,), (1,)), ((), ())), preferred_element_type=jnp.float32)
    start = jnp.sum(jnp.where(slab_of < iota((slabs, rows), 1), counts, 0.0), axis=0, keepdims=True)
    start = jnp.minimum(start.astype(jnp.int32) // ALIGN, (rows - window) // ALIGN).astype(jnp.float32)
    meta = jnp.where(iota((16, rows), 0) == 10, start, ordered).astype(jnp.bfloat16)
    return order, meta


def piece_of(x_ref, column, width):
    if len(x_ref.shape) == 3:
        return x_ref[column]
    return x_ref[:, pl.ds(pl.multiple_of(column * width, width), width)]


def by_slab(x, slabs, width):
    if width % LANES == 0:
        return x
    return x.reshape(x.shape[0], -1, width).transpose(1, 0, 2)


def sorted_piece(order, x_ref, column, width):
    piece = piece_of(x_ref, column, width)
    return jnp.dot(order, piece, preferred_element_type=jnp.float32).astype(jnp.bfloat16)


def plan_kernel(slabs, window, width, me_ref, *refs):
    ids_refs, table_ref, x_refs, order_ref, out_refs = refs[0:2], refs[2], refs[3:5], refs[5], refs[6:]
    rows = order_ref.shape[1]
    lines = 16 * (rows // width)
    for half in range(2):
        ids = ids_refs[half][...]
        order, meta = plan(slabs, window, ids[0:1], ids[1:2], ids[2:3], table_ref[...])
        order_ref[half] = order
        for i, out in enumerate(out_refs):
            column = jnp.bitwise_xor(me_ref[0], 2 * i)
            out[half * rows : (half + 1) * rows, :] = sorted_piece(order, x_refs[half], column, width)
            for j in range(rows // width):
                at = 2 * rows + half * lines + 16 * j
                out[at : at + 16, :] = meta[:, j * width : (j + 1) * width]


def plan_rows(slabs, window, me, ids, table, xs):
    rows, kx = xs[0].shape
    width = kx // slabs
    out = jax.ShapeDtypeStruct((2 * rows + 32 * (rows // width), width), jnp.bfloat16)
    done = pl.pallas_call(
        functools.partial(plan_kernel, slabs, window, width),
        out_shape=[jax.ShapeDtypeStruct((2, rows, rows), jnp.bfloat16)] + [out] * (slabs // 2),
        in_specs=[SCALARS] + [WHOLE] * 5,
        out_specs=[WHOLE] * (1 + slabs // 2),
        compiler_params=params(width),
        cost_estimate=cost(6.0),
        name="plan_rows",
    )(me, *[far(x) for x in ids], far(table.T), *[far(by_slab(x, slabs, width)) for x in xs])
    return done[0], done[1:]


def sort_kernel(slabs, width, part, ties, me_ref, order_ref, *refs):
    x_refs, out_refs = refs[0:2], refs[2 + ties :]
    rows = order_ref.shape[1]
    for i, out in enumerate(out_refs):
        column = jnp.bitwise_xor(me_ref[0], 2 * i) + part * slabs
        for half in range(2):
            out[half * rows : (half + 1) * rows, :] = sorted_piece(order_ref[half], x_refs[half], column, width)


def sort_columns(slabs, me, order, xs, part, ties):
    rows, kx = order.shape[1], xs[0].shape[1] // 2
    width = kx // slabs
    if width % LANES == 0:
        x_spec = pl.BlockSpec((rows, kx), functools.partial(lambda part, i, s: (0, part), part))
        part = 0
    else:
        x_spec = pl.BlockSpec((2 * slabs, rows, width), lambda i, s: (0, 0, 0))
    out = pl.BlockSpec((2 * rows, width), lambda i, s: (0, 0))
    return pl.pallas_call(
        functools.partial(sort_kernel, slabs, width, part, len(ties)),
        out_shape=[jax.ShapeDtypeStruct((2 * rows, width), jnp.bfloat16)] * (slabs // 2),
        grid_spec=pltpu.PrefetchScalarGridSpec(
            num_scalar_prefetch=1,
            grid=(1,),
            in_specs=[pl.BlockSpec(order.shape, lambda i, s: (0, 0, 0)), x_spec, x_spec] + [UNREAD] * len(ties),
            out_specs=[out] * (slabs // 2),
        ),
        compiler_params=params(width),
        cost_estimate=cost(3.0),
        name="sort_columns",
    )(me, order, *[far(by_slab(x, slabs, width)) for x in xs], *ties)


def swap(x, slabs, offset):
    return lax.ppermute(x, "slab", [(i, i ^ offset) for i in range(slabs)])


def exchange(pieces):
    return [pieces[0]] + [swap(pieces[i], 2 * len(pieces), 2 * i) for i in range(1, len(pieces))]


def volume_kernel(slabs, window, messages, first, ties, idx_ref, *refs):
    refs = refs[ties:]
    piece_refs, refs = refs[: slabs // 2], refs[slabs // 2 :]
    if first:
        sums_ref, meta_ref, code_refs = refs[0], refs[1], refs[2:-4]
    else:
        meta_ref, sums_ref, code_refs = refs[0], refs[1], refs[2:-4]
    all_ref, line_ref, scalar_ref, sem = refs[-4:]
    width = sums_ref.shape[3]
    rows = all_ref.shape[1]
    pick = (iota((16, LANES), 0) == iota((16, LANES), 1)).astype(jnp.bfloat16)
    for offset in range(slabs):
        if first:
            for i in range(rows // width):
                at = 2 * rows + 16 * (offset % 2 * (rows // width) + i)
                meta_ref[offset, :, i * width : (i + 1) * width] = piece_refs[offset // 2][at : at + 16, :]
        meta = meta_ref[offset]
        all_ref[offset] = lax.dot_general(
            meta, pick, (((0,), (0,)), ((), ())), preferred_element_type=jnp.float32
        ).astype(jnp.bfloat16)
        line_ref[offset : offset + 1, :] = meta.astype(jnp.float32)[10:11, 0:LANES].astype(jnp.int32) * ALIGN
    copy = pltpu.make_async_copy(line_ref, scalar_ref, sem)
    copy.start()
    copy.wait()

    def slab_sums(slab):
        about, here = [], []
        for offset in range(slabs):
            start = pl.multiple_of(scalar_ref[offset, slab], ALIGN)
            about.append(all_ref[offset, pl.ds(start, window), :])
            start = pl.multiple_of(offset % 2 * rows + start, ALIGN)
            here.append(piece_refs[offset // 2][pl.ds(start, window), :])
        about, here = jnp.concatenate(about, axis=0), jnp.concatenate(here, axis=0)
        meta = lax.dot_general(pick, about, (((1,), (1,)), ((), ())), preferred_element_type=jnp.float32)
        weights = meta[0:8]
        own = meta[8:9] == jnp.asarray(slab, jnp.float32)
        block = jnp.broadcast_to(jnp.where(own, meta[9:10], -1.0), weights.shape)
        spread = jnp.concatenate([jnp.where(block == float(b), weights, 0.0) for b in range(NBLK)], axis=0)
        sums = jnp.dot(spread.astype(jnp.bfloat16), here, preferred_element_type=jnp.float32)
        sums_ref[:, slab] = sums.reshape(YWIN, KZ_DEV, width)

    if slabs <= 8:
        for slab in range(slabs):
            slab_sums(slab)
    else:
        lax.fori_loop(0, slabs, lambda slab, carry: (slab_sums(slab), carry)[1], 0)
    portion = code_refs[0].shape[1] - ALIGN
    lines = portion // (slabs * KZ_DEV)
    at = 0
    for code_ref, count in zip(code_refs, messages):
        for i in range(count):
            x = sums_ref[pl.ds(idx_ref[at] * lines, lines)].reshape(portion, width)
            code_ref[i, :portion, :], code_ref[i, portion:, :] = encode(x)
            at += 1


def volume_sums(window, index, messages, groups, pieces, meta, ties):
    slabs = 2 * len(pieces)
    width = pieces[0].shape[1]
    first = meta is None
    rows = pieces[0].shape[0] // 2
    if first:
        rows = rows * width // (width + 16)
    portion = YWIN // groups * slabs * KZ_DEV
    out_shape = [
        jax.ShapeDtypeStruct((YWIN, slabs, KZ_DEV, width), jnp.float32),
    ]
    if first:
        out_shape.append(jax.ShapeDtypeStruct((slabs, 16, rows), jnp.bfloat16))
    out_shape += [jax.ShapeDtypeStruct((count, portion + ALIGN, width), jnp.int16) for count in messages]
    done = pl.pallas_call(
        functools.partial(volume_kernel, slabs, window, messages, first, len(ties)),
        out_shape=out_shape,
        in_specs=[SCALARS] + [UNREAD] * len(ties) + [WHOLE] * (len(pieces) + (0 if first else 1)),
        out_specs=[WHOLE] * len(out_shape),
        scratch_shapes=[
            pltpu.VMEM((slabs, rows, LANES), jnp.bfloat16),
            pltpu.VMEM((slabs, LANES), jnp.int32),
            pltpu.SMEM((slabs, LANES), jnp.int32),
            pltpu.SemaphoreType.DMA,
        ],
        compiler_params=params(width),
        cost_estimate=cost(7.0),
        name="volume_sums",
    )(index, *ties, *[far(x) for x in pieces], *([] if first else [meta]))
    sums = done[0].reshape(groups, portion, width)
    return (sums, done[2:], done[1]) if first else (sums, done[1:], meta)


def encode(x):
    rows, width = x.shape
    groups = rows // 8
    tiles = x.reshape(groups, 8, width)
    size = jnp.abs(tiles)
    most = jnp.max(jnp.max(size, axis=1), axis=1, keepdims=True)
    level = jnp.ceil(jnp.log2(jnp.maximum(most, 1e-30)) * STEPS) + 1.0
    inverse = jnp.broadcast_to(jnp.exp2(level * (-1.0 / STEPS)), (groups, width)).reshape(groups, 1, width)
    share = jnp.maximum(size * inverse, 1e-12)
    root = jnp.minimum(share * lax.rsqrt(share) * TOP + 0.5, TOP)
    code = jnp.where(tiles < 0, -root, root).reshape(rows, width).astype(jnp.int32).astype(jnp.int16)
    eye = iota((width, width), 0) == iota((width, width), 1)
    lines = [
        jnp.sum(jnp.where(eye, level[i * width : (i + 1) * width], 0.0), axis=0, keepdims=True)
        for i in range(groups // width)
    ]
    lines.append(jnp.zeros((ALIGN - len(lines), width), jnp.float32))
    return code, jnp.concatenate(lines, axis=0).astype(jnp.int32).astype(jnp.int16)


def decode(code, lines):
    rows, width = code.shape
    groups = rows // 8
    x = code.astype(jnp.int32).astype(jnp.float32)
    lines = lines.astype(jnp.int32).astype(jnp.float32)
    eye = iota((width, width), 0) == iota((width, width), 1)
    level = jnp.concatenate(
        [jnp.sum(jnp.where(eye, lines[i : i + 1], 0.0), axis=1, keepdims=True) for i in range(groups // width)],
        axis=0,
    )
    scale = jnp.exp2(level * (1.0 / STEPS)) * (1.0 / (TOP * TOP))
    scale = jnp.broadcast_to(scale, (groups, width)).reshape(groups, 1, width)
    return ((x * jnp.abs(x)).reshape(groups, 8, width) * scale).reshape(rows, width)


def hop_kernel(places, idx_ref, sums_ref, prev_ref, out_ref):
    rows = sums_ref.shape[1]
    for i, place in enumerate(places):
        x = sums_ref[idx_ref[i]] + decode(prev_ref[place, :rows, :], prev_ref[place, rows:, :])
        out_ref[i, :rows, :], out_ref[i, rows:, :] = encode(x)


def hop(index, sums, prev, places):
    _, rows, width = sums.shape
    count = len(places)
    return pl.pallas_call(
        functools.partial(hop_kernel, places),
        out_shape=jax.ShapeDtypeStruct((count, rows + ALIGN, width), jnp.int16),
        in_specs=[SCALARS, WHOLE, WHOLE],
        out_specs=WHOLE,
        compiler_params=params(width),
        cost_estimate=cost(2.0 + count),
        name="hop",
    )(index, sums, prev)


def portions(z, groups, r):
    return jnp.where(z >= groups // 2, groups - 1 - r, r).astype(jnp.int32)


def along_z(sums, messages, payloads, z, groups, split):
    half = groups // 2
    depth = jnp.minimum(z, groups - 1 - z)

    def send(payload, pairs):
        return lax.ppermute(payload, "grp", pairs + [(groups - 1 - a, groups - 1 - b) for a, b in pairs])

    def cut(rs):
        return [[r] for r in rs] if split else [list(rs)]

    def add(rs, got):
        return hop(portions(z, groups, np.array(rs)), sums, got[rs[0]][0], [got[r][1] for r in rs])

    def step(rs, got, pairs):
        new = {}
        for part in cut(rs):
            payload = send(add(part, got), pairs)
            new.update({r: (payload, i) for i, r in enumerate(part)})
        return new

    got = {}
    for part, payload in zip(messages, payloads):
        payload = send(payload, [(0, 1)])
        got.update({r: (payload, i) for i, r in enumerate(part)})
    inward = [None, got]
    for k in range(2, half):
        got = step(range(groups - 1, k, -1), got, [(k - 1, k)])
        inward.append(got)
    got = step(range(groups - 1, half - 1, -1), got, [(half - 1, half)])
    got = {groups - 1 - r: x for r, x in got.items()}
    ends = [got[half - 1]]
    for j in range(half - 1, 1, -1):
        ends.append((send(add([j], inward[j - 1]), [(j - 1, j)]), 0))
        got = step(range(j), got, [(j, j - 1)])
        ends.append(got[j - 1])
    last = jnp.where(depth == 0, 1, 0).reshape(1)
    payload = hop(portions(z, groups, last), sums, got[0][0], [got[0][1]])
    ends.append((send(payload, [(1, 0), (0, 1)]), 0))
    return ends


def image_kernel(parts, zs, own_ref, *refs):
    tau_ref, high_ref, low_ref, out_ref = refs[-4:]
    each = len(refs[:-4]) // 3
    volume = []
    for c in range(3):
        sums_ref, coded = refs[c * each], refs[c * each + 1 : (c + 1) * each]
        rows = sums_ref.shape[1]
        x = sums_ref[0]
        for ref in coded:
            x = x + decode(ref[0, :rows, :], ref[0, rows:, :])
        volume.append(x)
    below = volume[2] + tau_ref[...]
    columns = []
    for c in range(2):
        x = volume[c] / below
        columns += [x[k * zs : (k + 1) * zs] for k in range(parts)]
    x = jnp.concatenate(columns, axis=1)
    x_high = x.astype(jnp.bfloat16)
    x_low = (x - x_high.astype(jnp.float32)).astype(jnp.bfloat16)
    dot = functools.partial(jnp.dot, preferred_element_type=jnp.float32)
    y = dot(high_ref[...], x_high) + (dot(high_ref[...], x_low) + dot(low_ref[...], x_high))
    span = x.shape[1] // 2
    width = span // parts
    real = y[:zs, :span] - y[zs:, span:]
    imag = y[zs:, :span] + y[:zs, span:]
    for k in range(parts):
        out_ref[0, k] = real[:, k * width : (k + 1) * width]
        out_ref[1, k] = imag[:, k * width : (k + 1) * width]


def image_of(own, fields, tau, zs):
    rows, width = fields[0][0].shape[1:]
    parts = rows // zs
    operands, specs = [], []
    for sums, ends in fields:
        operands.append(sums)
        specs.append(pl.BlockSpec((1, rows, width), lambda i, s: (s[0], 0, 0)))
        for payload, place in ends:
            operands.append(payload)
            specs.append(pl.BlockSpec((1, rows + ALIGN, width), functools.partial(lambda place, i, s: (place, 0, 0), place)))
    steps = np.arange(zs)
    angles = (steps[:, None] * steps[None, :] % zs) * (2.0 * math.pi / zs)
    table = (np.concatenate([np.cos(angles), np.sin(angles)], axis=0) / math.sqrt(zs)).astype(np.float32)
    high = table.astype(jnp.bfloat16)
    low = (table - high.astype(np.float32)).astype(jnp.bfloat16)
    for x in (tau.reshape(1, width), jnp.asarray(high), jnp.asarray(low)):
        operands.append(x)
        specs.append(pl.BlockSpec(x.shape, lambda i, s: (0, 0)))
    return pl.pallas_call(
        functools.partial(image_kernel, parts, zs),
        out_shape=jax.ShapeDtypeStruct((2, parts, zs, width), jnp.float32),
        grid_spec=pltpu.PrefetchScalarGridSpec(
            num_scalar_prefetch=1,
            grid=(1,),
            in_specs=specs,
            out_specs=pl.BlockSpec((2, parts, zs, width), lambda i, s: (0, 0, 0, 0)),
        ),
        compiler_params=params(width),
        cost_estimate=cost(6.0),
        name="image_of",
    )(own, *[far(x) for x in operands])


def on_device(spectra, ctf_sq, dest, block, pattern, pattern_table, tau):
    slabs, groups = lax.axis_size("slab"), lax.axis_size("grp")
    rows, kx = ctf_sq.shape
    capacity = max(2, 2 * rows // slabs)
    window = min(rows, -(-capacity // ALIGN) * ALIGN + ALIGN)
    width = kx // slabs
    slab, z = lax.axis_index("slab"), lax.axis_index("grp")
    me = slab.astype(jnp.int32).reshape(1)
    ids = jnp.stack([dest[:, 0], block, pattern])
    ids, ctf_sq, spectra = [(x, swap(x, slabs, 1)) for x in (ids, ctf_sq, spectra)]
    order, ctf = plan_rows(slabs, window, me, ids, pattern_table, ctf_sq)
    first = list(range(groups - 1, 1, -1))
    index = portions(z, groups, np.array(first))

    def volume(piece, meta, ties, split):
        messages = [[r] for r in first] if split else [first]
        sums, payloads, meta = volume_sums(window, index, [len(x) for x in messages], groups, piece, meta, ties)
        return (sums, messages, payloads, z, groups, split), payloads[0], meta

    real = sort_columns(slabs, me, order, spectra, 0, ())
    ctf, real_there = exchange(ctf), exchange(real)
    ctf_part, ctf_code, meta = volume(ctf, None, (real[0],), True)
    imag = sort_columns(slabs, me, order, spectra, 1, (ctf_code, real_there[1]))
    imag_there = exchange(imag)
    real_part, real_code, _ = volume(real_there, meta, (imag[0],), True)
    imag_part, imag_code, _ = volume(imag_there, meta, (real_code,), True)
    fields = [(part[0], along_z(*part)) for part in (ctf_part, real_part, imag_part)]
    tau_here = lax.dynamic_slice_in_dim(tau, slab * width, width, 0)
    own = z.astype(jnp.int32).reshape(1)
    return image_of(own, [fields[1], fields[2], fields[0]], tau_here, KZ_DEV * slabs)


def solution(mesh):
    in_specs = (
        P(("grp", "slab"), None),
        P(("grp", "slab"), None),
        P(("grp", "slab"), None),
        P(("grp", "slab")),
        P(("grp", "slab")),
        P(),
        P(),
    )
    out_specs = P(None, "grp", None, "slab")
    return jax.shard_map(
        on_device, mesh=mesh, in_specs=in_specs, out_specs=out_specs, check_vma=False
    )
```

```python
import functools
import math

import jax
import jax.numpy as jnp
import numpy as np
from jax import lax
from jax.experimental import pallas as pl
from jax.experimental.pallas import tpu as pltpu
from jax.sharding import PartitionSpec as P

KZ_DEV = 32
YWIN = 16
NBLK = 64
LANES = 128
ALIGN = 16
TOP = 32767.0
STEPS = 256.0
VMEM = 60 * 1024 * 1024

WHOLE = pl.BlockSpec(memory_space=pltpu.VMEM)
SCALARS = pl.BlockSpec(memory_space=pltpu.SMEM)
UNREAD = pl.BlockSpec(memory_space=pl.ANY)


def params(width):
    return pltpu.CompilerParams(vmem_limit_bytes=VMEM if width < LANES else VMEM // 2)


def far(x):
    return pltpu.with_memory_space_constraint(x, pltpu.HBM)


def cost(micros):
    return pl.CostEstimate(flops=0, bytes_accessed=int(micros * 3.0e6), transcendentals=0)


def iota(shape, axis):
    return lax.broadcasted_iota(jnp.int32, shape, axis)


def plan(slabs, window, dest, block, pattern, table):
    rows = dest.shape[1]
    mine = (dest == iota((slabs, rows), 0)).astype(jnp.float32)
    before = (iota((rows, rows), 0) < iota((rows, rows), 1)).astype(jnp.bfloat16)
    rank = jnp.dot(mine.astype(jnp.bfloat16), before, preferred_element_type=jnp.float32)
    counts = jnp.sum(mine, axis=1, keepdims=True)
    slab_of = iota((slabs, rows), 0)
    first = jnp.sum(jnp.where(slab_of < dest, counts, 0.0), axis=0, keepdims=True)
    target = (first + jnp.sum(mine * rank, axis=0, keepdims=True)).astype(jnp.int32)
    order = (target == iota((rows, rows), 0)).astype(jnp.bfloat16)
    ids = (pattern == iota((table.shape[1], rows), 0)).astype(jnp.bfloat16)
    weights = jnp.dot(table, ids, preferred_element_type=jnp.float32)
    line = iota((8, rows), 0)
    named = jnp.where(line == 0, dest, jnp.where(line == 1, block, 0)).astype(jnp.float32)
    given = jnp.concatenate([weights, named], axis=0).astype(jnp.bfloat16)
    ordered = lax.dot_general(given, order, (((1,), (1,)), ((), ())), preferred_element_type=jnp.float32)
    start = jnp.sum(jnp.where(slab_of < iota((slabs, rows), 1), counts, 0.0), axis=0, keepdims=True)
    start = jnp.minimum(start.astype(jnp.int32) // ALIGN, (rows - window) // ALIGN).astype(jnp.float32)
    meta = jnp.where(iota((16, rows), 0) == 10, start, ordered).astype(jnp.bfloat16)
    return order, meta


def piece_of(x_ref, column, width):
    if len(x_ref.shape) == 3:
        return x_ref[column]
    return x_ref[:, pl.ds(pl.multiple_of(column * width, width), width)]


def by_slab(x, slabs, width):
    if width % LANES == 0:
        return x
    return x.reshape(x.shape[0], -1, width).transpose(1, 0, 2)


def sorted_piece(order, x_ref, column, width):
    piece = piece_of(x_ref, column, width)
    return jnp.dot(order, piece, preferred_element_type=jnp.float32).astype(jnp.bfloat16)


def plan_kernel(slabs, window, width, me_ref, *refs):
    ids_refs, table_ref, x_refs, order_ref, out_refs = refs[0:2], refs[2], refs[3:5], refs[5], refs[6:]
    rows = order_ref.shape[1]
    lines = 16 * (rows // width)
    for half in range(2):
        ids = ids_refs[half][...]
        order, meta = plan(slabs, window, ids[0:1], ids[1:2], ids[2:3], table_ref[...])
        order_ref[half] = order
        for i, out in enumerate(out_refs):
            column = jnp.bitwise_xor(me_ref[0], 2 * i)
            out[half * rows : (half + 1) * rows, :] = sorted_piece(order, x_refs[half], column, width)
            for j in range(rows // width):
                at = 2 * rows + half * lines + 16 * j
                out[at : at + 16, :] = meta[:, j * width : (j + 1) * width]


def plan_rows(slabs, window, me, ids, table, xs):
    rows, kx = xs[0].shape
    width = kx // slabs
    out = jax.ShapeDtypeStruct((2 * rows + 32 * (rows // width), width), jnp.bfloat16)
    done = pl.pallas_call(
        functools.partial(plan_kernel, slabs, window, width),
        out_shape=[jax.ShapeDtypeStruct((2, rows, rows), jnp.bfloat16)] + [out] * (slabs // 2),
        in_specs=[SCALARS] + [WHOLE] * 5,
        out_specs=[WHOLE] * (1 + slabs // 2),
        compiler_params=params(width),
        cost_estimate=cost(6.0),
        name="plan_rows",
    )(me, *[far(x) for x in ids], far(table.T), *[far(by_slab(x, slabs, width)) for x in xs])
    return done[0], done[1:]


def sort_kernel(slabs, width, part, ties, me_ref, order_ref, *refs):
    x_refs, out_refs = refs[0:2], refs[2 + ties :]
    rows = order_ref.shape[1]
    for i, out in enumerate(out_refs):
        column = jnp.bitwise_xor(me_ref[0], 2 * i) + part * slabs
        for half in range(2):
            out[half * rows : (half + 1) * rows, :] = sorted_piece(order_ref[half], x_refs[half], column, width)


def sort_columns(slabs, me, order, xs, part, ties):
    rows, kx = order.shape[1], xs[0].shape[1] // 2
    width = kx // slabs
    if width % LANES == 0:
        x_spec = pl.BlockSpec((rows, kx), functools.partial(lambda part, i, s: (0, part), part))
        part = 0
    else:
        x_spec = pl.BlockSpec((2 * slabs, rows, width), lambda i, s: (0, 0, 0))
    out = pl.BlockSpec((2 * rows, width), lambda i, s: (0, 0))
    return pl.pallas_call(
        functools.partial(sort_kernel, slabs, width, part, len(ties)),
        out_shape=[jax.ShapeDtypeStruct((2 * rows, width), jnp.bfloat16)] * (slabs // 2),
        grid_spec=pltpu.PrefetchScalarGridSpec(
            num_scalar_prefetch=1,
            grid=(1,),
            in_specs=[pl.BlockSpec(order.shape, lambda i, s: (0, 0, 0)), x_spec, x_spec] + [UNREAD] * len(ties),
            out_specs=[out] * (slabs // 2),
        ),
        compiler_params=params(width),
        cost_estimate=cost(3.0),
        name="sort_columns",
    )(me, order, *[far(by_slab(x, slabs, width)) for x in xs], *ties)


def swap(x, slabs, offset):
    return lax.ppermute(x, "slab", [(i, i ^ offset) for i in range(slabs)])


def exchange(pieces):
    return [pieces[0]] + [swap(pieces[i], 2 * len(pieces), 2 * i) for i in range(1, len(pieces))]


def volume_kernel(slabs, window, messages, first, ties, idx_ref, *refs):
    refs = refs[ties:]
    piece_refs, refs = refs[: slabs // 2], refs[slabs // 2 :]
    if first:
        sums_ref, meta_ref, code_refs = refs[0], refs[1], refs[2:-4]
    else:
        meta_ref, sums_ref, code_refs = refs[0], refs[1], refs[2:-4]
    all_ref, line_ref, scalar_ref, sem = refs[-4:]
    width = sums_ref.shape[3]
    rows = all_ref.shape[1]
    pick = (iota((16, LANES), 0) == iota((16, LANES), 1)).astype(jnp.bfloat16)
    for offset in range(slabs):
        if first:
            for i in range(rows // width):
                at = 2 * rows + 16 * (offset % 2 * (rows // width) + i)
                meta_ref[offset, :, i * width : (i + 1) * width] = piece_refs[offset // 2][at : at + 16, :]
        meta = meta_ref[offset]
        all_ref[offset] = lax.dot_general(
            meta, pick, (((0,), (0,)), ((), ())), preferred_element_type=jnp.float32
        ).astype(jnp.bfloat16)
        line_ref[offset : offset + 1, :] = meta.astype(jnp.float32)[10:11, 0:LANES].astype(jnp.int32) * ALIGN
    copy = pltpu.make_async_copy(line_ref, scalar_ref, sem)
    copy.start()
    copy.wait()

    def slab_sums(slab):
        about, here = [], []
        for offset in range(slabs):
            start = pl.multiple_of(scalar_ref[offset, slab], ALIGN)
            about.append(all_ref[offset, pl.ds(start, window), :])
            start = pl.multiple_of(offset % 2 * rows + start, ALIGN)
            here.append(piece_refs[offset // 2][pl.ds(start, window), :])
        about, here = jnp.concatenate(about, axis=0), jnp.concatenate(here, axis=0)
        meta = lax.dot_general(pick, about, (((1,), (1,)), ((), ())), preferred_element_type=jnp.float32)
        weights = meta[0:8]
        own = meta[8:9] == jnp.asarray(slab, jnp.float32)
        block = jnp.broadcast_to(jnp.where(own, meta[9:10], -1.0), weights.shape)
        spread = jnp.concatenate([jnp.where(block == float(b), weights, 0.0) for b in range(NBLK)], axis=0)
        sums = jnp.dot(spread.astype(jnp.bfloat16), here, preferred_element_type=jnp.float32)
        sums_ref[:, slab] = sums.reshape(YWIN, KZ_DEV, width)

    if slabs <= 8:
        for slab in range(slabs):
            slab_sums(slab)
    else:
        lax.fori_loop(0, slabs, lambda slab, carry: (slab_sums(slab), carry)[1], 0)
    portion = code_refs[0].shape[1] - ALIGN
    lines = portion // (slabs * KZ_DEV)
    at = 0
    for code_ref, count in zip(code_refs, messages):
        for i in range(count):
            x = sums_ref[pl.ds(idx_ref[at] * lines, lines)].reshape(portion, width)
            code_ref[i, :portion, :], code_ref[i, portion:, :] = encode(x)
            at += 1


def volume_sums(window, index, messages, groups, pieces, meta, ties):
    slabs = 2 * len(pieces)
    width = pieces[0].shape[1]
    first = meta is None
    rows = pieces[0].shape[0] // 2
    if first:
        rows = rows * width // (width + 16)
    portion = YWIN // groups * slabs * KZ_DEV
    out_shape = [
        jax.ShapeDtypeStruct((YWIN, slabs, KZ_DEV, width), jnp.float32),
    ]
    if first:
        out_shape.append(jax.ShapeDtypeStruct((slabs, 16, rows), jnp.bfloat16))
    out_shape += [jax.ShapeDtypeStruct((count, portion + ALIGN, width), jnp.int16) for count in messages]
    done = pl.pallas_call(
        functools.partial(volume_kernel, slabs, window, messages, first, len(ties)),
        out_shape=out_shape,
        in_specs=[SCALARS] + [UNREAD] * len(ties) + [WHOLE] * (len(pieces) + (0 if first else 1)),
        out_specs=[WHOLE] * len(out_shape),
        scratch_shapes=[
            pltpu.VMEM((slabs, rows, LANES), jnp.bfloat16),
            pltpu.VMEM((slabs, LANES), jnp.int32),
            pltpu.SMEM((slabs, LANES), jnp.int32),
            pltpu.SemaphoreType.DMA,
        ],
        compiler_params=params(width),
        cost_estimate=cost(7.0),
        name="volume_sums",
    )(index, *ties, *[far(x) for x in pieces], *([] if first else [meta]))
    sums = done[0].reshape(groups, portion, width)
    return (sums, done[2:], done[1]) if first else (sums, done[1:], meta)


def encode(x):
    rows, width = x.shape
    groups = rows // 8
    tiles = x.reshape(groups, 8, width)
    size = jnp.abs(tiles)
    most = jnp.max(jnp.max(size, axis=1), axis=1, keepdims=True)
    level = jnp.ceil(jnp.log2(jnp.maximum(most, 1e-30)) * STEPS) + 1.0
    inverse = jnp.broadcast_to(jnp.exp2(level * (-1.0 / STEPS)), (groups, width)).reshape(groups, 1, width)
    share = jnp.maximum(size * inverse, 1e-12)
    root = jnp.minimum(share * lax.rsqrt(share) * TOP + 0.5, TOP)
    code = jnp.where(tiles < 0, -root, root).reshape(rows, width).astype(jnp.int32).astype(jnp.int16)
    eye = iota((width, width), 0) == iota((width, width), 1)
    lines = [
        jnp.sum(jnp.where(eye, level[i * width : (i + 1) * width], 0.0), axis=0, keepdims=True)
        for i in range(groups // width)
    ]
    lines.append(jnp.zeros((ALIGN - len(lines), width), jnp.float32))
    return code, jnp.concatenate(lines, axis=0).astype(jnp.int32).astype(jnp.int16)


def decode(code, lines):
    rows, width = code.shape
    groups = rows // 8
    x = code.astype(jnp.int32).astype(jnp.float32)
    lines = lines.astype(jnp.int32).astype(jnp.float32)
    eye = iota((width, width), 0) == iota((width, width), 1)
    level = jnp.concatenate(
        [jnp.sum(jnp.where(eye, lines[i : i + 1], 0.0), axis=1, keepdims=True) for i in range(groups // width)],
        axis=0,
    )
    scale = jnp.exp2(level * (1.0 / STEPS)) * (1.0 / (TOP * TOP))
    scale = jnp.broadcast_to(scale, (groups, width)).reshape(groups, 1, width)
    return ((x * jnp.abs(x)).reshape(groups, 8, width) * scale).reshape(rows, width)


def hop_kernel(places, idx_ref, sums_ref, prev_ref, *refs):
    out_ref = refs[-1]
    rows = sums_ref.shape[1]
    for i, place in enumerate(places):
        x = sums_ref[idx_ref[i]] + decode(prev_ref[place, :rows, :], prev_ref[place, rows:, :])
        out_ref[i, :rows, :], out_ref[i, rows:, :] = encode(x)


def hop(index, sums, prev, places, ties):
    _, rows, width = sums.shape
    count = len(places)
    return pl.pallas_call(
        functools.partial(hop_kernel, places),
        out_shape=jax.ShapeDtypeStruct((count, rows + ALIGN, width), jnp.int16),
        in_specs=[SCALARS, WHOLE, WHOLE] + [UNREAD] * len(ties),
        out_specs=WHOLE,
        compiler_params=params(width),
        cost_estimate=cost(2.0 + count),
        name="hop",
    )(index, sums, prev, *ties)


def portions(z, groups, r):
    return jnp.where(z >= groups // 2, groups - 1 - r, r).astype(jnp.int32)


class AlongZ:
    def __init__(self, sums, first, payloads, z, groups):
        self.sums, self.z, self.groups, self.ends = sums, z, groups, []
        half = groups // 2
        got = [{r: self.send(x, [(0, 1)]) for r, x in zip(first, payloads)}]
        hops = []
        for k in range(2, half):
            got.append({})
            for r in range(groups - 1, k, -1):
                hops.append(functools.partial(self.move, got[k - 2], r, got[k - 1], r, [(k - 1, k)]))
        across = {}
        for r in range(groups - 1, half - 1, -1):
            hops.append(functools.partial(self.move, got[half - 2], r, across, groups - 1 - r, [(half - 1, half)]))
        outward = across
        for j in range(half - 1, 1, -1):
            kept, new = {}, {}
            hops.append(functools.partial(self.move, got[j - 2], j, kept, j, [(j - 1, j)], True))
            for r in range(j):
                hops.append(functools.partial(self.move, outward, r, new, r, [(j, j - 1)], r == j - 1))
            outward = new
        hops.append(functools.partial(self.move, outward, 0, {}, 0, [(1, 0), (0, 1)], True, True))
        self.hops, self.keep = hops, half - 1

    def send(self, payload, pairs):
        last = self.groups - 1
        return lax.ppermute(payload, "grp", pairs + [(last - a, last - b) for a, b in pairs])

    def move(self, source, r, target, place, pairs, final=False, both=False, ties=()):
        last = self.groups - 1
        wanted = jnp.full((1,), r, jnp.int32)
        if both:
            wanted = jnp.where(jnp.minimum(self.z, last - self.z) == 0, 1, 0).astype(jnp.int32).reshape(1)
        payload = hop(portions(self.z, self.groups, wanted), self.sums, source[r], [0], ties)
        target[place] = self.send(payload, pairs)
        if final or (len(pairs) == 1 and pairs[0] == (self.keep, self.keep + 1) and place == self.keep):
            self.ends.append((target[place], 0))
        return payload


def image_kernel(parts, zs, own_ref, *refs):
    tau_ref, high_ref, low_ref, out_ref = refs[-4:]
    each = len(refs[:-4]) // 3
    volume = []
    for c in range(3):
        sums_ref, coded = refs[c * each], refs[c * each + 1 : (c + 1) * each]
        rows = sums_ref.shape[1]
        x = sums_ref[0]
        for ref in coded:
            x = x + decode(ref[0, :rows, :], ref[0, rows:, :])
        volume.append(x)
    below = volume[2] + tau_ref[...]
    columns = []
    for c in range(2):
        x = volume[c] / below
        columns += [x[k * zs : (k + 1) * zs] for k in range(parts)]
    x = jnp.concatenate(columns, axis=1)
    x_high = x.astype(jnp.bfloat16)
    x_low = (x - x_high.astype(jnp.float32)).astype(jnp.bfloat16)
    dot = functools.partial(jnp.dot, preferred_element_type=jnp.float32)
    y = dot(high_ref[...], x_high) + (dot(high_ref[...], x_low) + dot(low_ref[...], x_high))
    span = x.shape[1] // 2
    width = span // parts
    real = y[:zs, :span] - y[zs:, span:]
    imag = y[zs:, :span] + y[:zs, span:]
    for k in range(parts):
        out_ref[0, k] = real[:, k * width : (k + 1) * width]
        out_ref[1, k] = imag[:, k * width : (k + 1) * width]


def image_of(own, fields, tau, zs):
    rows, width = fields[0][0].shape[1:]
    parts = rows // zs
    operands, specs = [], []
    for sums, ends in fields:
        operands.append(sums)
        specs.append(pl.BlockSpec((1, rows, width), lambda i, s: (s[0], 0, 0)))
        for payload, place in ends:
            operands.append(payload)
            specs.append(pl.BlockSpec((1, rows + ALIGN, width), functools.partial(lambda place, i, s: (place, 0, 0), place)))
    steps = np.arange(zs)
    angles = (steps[:, None] * steps[None, :] % zs) * (2.0 * math.pi / zs)
    table = (np.concatenate([np.cos(angles), np.sin(angles)], axis=0) / math.sqrt(zs)).astype(np.float32)
    high = table.astype(jnp.bfloat16)
    low = (table - high.astype(np.float32)).astype(jnp.bfloat16)
    for x in (tau.reshape(1, width), jnp.asarray(high), jnp.asarray(low)):
        operands.append(x)
        specs.append(pl.BlockSpec(x.shape, lambda i, s: (0, 0)))
    return pl.pallas_call(
        functools.partial(image_kernel, parts, zs),
        out_shape=jax.ShapeDtypeStruct((2, parts, zs, width), jnp.float32),
        grid_spec=pltpu.PrefetchScalarGridSpec(
            num_scalar_prefetch=1,
            grid=(1,),
            in_specs=specs,
            out_specs=pl.BlockSpec((2, parts, zs, width), lambda i, s: (0, 0, 0, 0)),
        ),
        compiler_params=params(width),
        cost_estimate=cost(6.0),
        name="image_of",
    )(own, *[far(x) for x in operands])


def on_device(spectra, ctf_sq, dest, block, pattern, pattern_table, tau):
    slabs, groups = lax.axis_size("slab"), lax.axis_size("grp")
    rows, kx = ctf_sq.shape
    capacity = max(2, 2 * rows // slabs)
    window = min(rows, -(-capacity // ALIGN) * ALIGN + ALIGN)
    width = kx // slabs
    slab, z = lax.axis_index("slab"), lax.axis_index("grp")
    me = slab.astype(jnp.int32).reshape(1)
    ids = jnp.stack([dest[:, 0], block, pattern])
    ids, ctf_sq, spectra = [(x, swap(x, slabs, 1)) for x in (ids, ctf_sq, spectra)]
    order, ctf = plan_rows(slabs, window, me, ids, pattern_table, ctf_sq)
    first = list(range(groups - 1, 1, -1))
    index = portions(z, groups, np.array(first))

    def volume(piece, meta, ties):
        sums, payloads, meta = volume_sums(window, index, [1] * len(first), groups, piece, meta, ties)
        return AlongZ(sums, first, payloads, z, groups), payloads[0], meta

    real = sort_columns(slabs, me, order, spectra, 0, ())
    ctf, real_there = exchange(ctf), exchange(real)
    ctf_part, coded, meta = volume(ctf, None, (real[0],))
    imag = sort_columns(slabs, me, order, spectra, 1, (real[0],))
    imag_there = exchange(imag)
    real_part, coded, _ = volume(real_there, meta, (imag[0],))
    tie = coded
    early = len(ctf_part.hops) - 1
    for step in ctf_part.hops[:early]:
        tie = step(ties=(tie,))
    imag_part, coded, _ = volume(imag_there, meta, (tie,))
    steps = real_part.hops[:-1] + ctf_part.hops[early:] + imag_part.hops[:1] + real_part.hops[-1:] + imag_part.hops[1:]
    tie = coded
    for step in steps:
        tie = step(ties=(tie,))
    fields = [(part.sums, part.ends) for part in (ctf_part, real_part, imag_part)]
    tau_here = lax.dynamic_slice_in_dim(tau, slab * width, width, 0)
    own = z.astype(jnp.int32).reshape(1)
    return image_of(own, [fields[1], fields[2], fields[0]], tau_here, KZ_DEV * slabs)


def solution(mesh):
    in_specs = (
        P(("grp", "slab"), None),
        P(("grp", "slab"), None),
        P(("grp", "slab"), None),
        P(("grp", "slab")),
        P(("grp", "slab")),
        P(),
        P(),
    )
    out_specs = P(None, "grp", None, "slab")
    return jax.shard_map(
        on_device, mesh=mesh, in_specs=in_specs, out_specs=out_specs, check_vma=False
    )
```

```python
import functools
import math

import jax
import jax.numpy as jnp
import numpy as np
from jax import lax
from jax.experimental import pallas as pl
from jax.experimental.pallas import tpu as pltpu
from jax.sharding import PartitionSpec as P

KZ_DEV = 32
YWIN = 16
NBLK = 64
LANES = 128
ALIGN = 16
TOP = 32767.0
STEPS = 256.0
VMEM = 60 * 1024 * 1024

WHOLE = pl.BlockSpec(memory_space=pltpu.VMEM)
SCALARS = pl.BlockSpec(memory_space=pltpu.SMEM)
UNREAD = pl.BlockSpec(memory_space=pl.ANY)


def params(width):
    return pltpu.CompilerParams(vmem_limit_bytes=VMEM if width < LANES else VMEM // 2)


def far(x):
    return pltpu.with_memory_space_constraint(x, pltpu.HBM)


def cost(micros):
    return pl.CostEstimate(flops=0, bytes_accessed=int(micros * 3.0e6), transcendentals=0)


def iota(shape, axis):
    return lax.broadcasted_iota(jnp.int32, shape, axis)


def plan(slabs, window, dest, block, pattern, table):
    rows = dest.shape[1]
    mine = (dest == iota((slabs, rows), 0)).astype(jnp.float32)
    before = (iota((rows, rows), 0) < iota((rows, rows), 1)).astype(jnp.bfloat16)
    rank = jnp.dot(mine.astype(jnp.bfloat16), before, preferred_element_type=jnp.float32)
    counts = jnp.sum(mine, axis=1, keepdims=True)
    slab_of = iota((slabs, rows), 0)
    first = jnp.sum(jnp.where(slab_of < dest, counts, 0.0), axis=0, keepdims=True)
    target = (first + jnp.sum(mine * rank, axis=0, keepdims=True)).astype(jnp.int32)
    order = (target == iota((rows, rows), 0)).astype(jnp.bfloat16)
    ids = (pattern == iota((table.shape[1], rows), 0)).astype(jnp.bfloat16)
    weights = jnp.dot(table, ids, preferred_element_type=jnp.float32)
    line = iota((8, rows), 0)
    named = jnp.where(line == 0, dest, jnp.where(line == 1, block, 0)).astype(jnp.float32)
    given = jnp.concatenate([weights, named], axis=0).astype(jnp.bfloat16)
    ordered = lax.dot_general(given, order, (((1,), (1,)), ((), ())), preferred_element_type=jnp.float32)
    start = jnp.sum(jnp.where(slab_of < iota((slabs, rows), 1), counts, 0.0), axis=0, keepdims=True)
    start = jnp.minimum(start.astype(jnp.int32) // ALIGN, (rows - window) // ALIGN).astype(jnp.float32)
    meta = jnp.where(iota((16, rows), 0) == 10, start, ordered).astype(jnp.bfloat16)
    return order, meta


def piece_of(x_ref, column, width):
    if len(x_ref.shape) == 3:
        return x_ref[column]
    return x_ref[:, pl.ds(pl.multiple_of(column * width, width), width)]


def by_slab(x, slabs, width):
    if width % LANES == 0:
        return x
    return x.reshape(x.shape[0], -1, width).transpose(1, 0, 2)


def sorted_piece(order, x_ref, column, width):
    piece = piece_of(x_ref, column, width)
    return jnp.dot(order, piece, preferred_element_type=jnp.float32).astype(jnp.bfloat16)


def plan_kernel(slabs, window, width, me_ref, *refs):
    ids_refs, table_ref, x_refs, order_ref, out_refs = refs[0:2], refs[2], refs[3:5], refs[5], refs[6:]
    rows = order_ref.shape[1]
    lines = 16 * (rows // width)
    for half in range(2):
        ids = ids_refs[half][...]
        order, meta = plan(slabs, window, ids[0:1], ids[1:2], ids[2:3], table_ref[...])
        order_ref[half] = order
        for i, out in enumerate(out_refs):
            column = jnp.bitwise_xor(me_ref[0], 2 * i)
            out[half * rows : (half + 1) * rows, :] = sorted_piece(order, x_refs[half], column, width)
            for j in range(rows // width):
                at = 2 * rows + half * lines + 16 * j
                out[at : at + 16, :] = meta[:, j * width : (j + 1) * width]


def plan_rows(slabs, window, me, ids, table, xs):
    rows, kx = xs[0].shape
    width = kx // slabs
    out = jax.ShapeDtypeStruct((2 * rows + 32 * (rows // width), width), jnp.bfloat16)
    done = pl.pallas_call(
        functools.partial(plan_kernel, slabs, window, width),
        out_shape=[jax.ShapeDtypeStruct((2, rows, rows), jnp.bfloat16)] + [out] * (slabs // 2),
        in_specs=[SCALARS] + [WHOLE] * 5,
        out_specs=[WHOLE] * (1 + slabs // 2),
        compiler_params=params(width),
        cost_estimate=cost(6.0),
        name="plan_rows",
    )(me, far(ids[0]), ids[1], far(table.T), far(by_slab(xs[0], slabs, width)), by_slab(xs[1], slabs, width))
    return done[0], done[1:]


def sort_kernel(slabs, width, part, ties, me_ref, order_ref, *refs):
    x_refs, out_refs = refs[0:2], refs[2 + ties :]
    rows = order_ref.shape[1]
    for i, out in enumerate(out_refs):
        column = jnp.bitwise_xor(me_ref[0], 2 * i) + part * slabs
        for half in range(2):
            out[half * rows : (half + 1) * rows, :] = sorted_piece(order_ref[half], x_refs[half], column, width)


def sort_columns(slabs, me, order, xs, part, ties):
    rows, kx = order.shape[1], xs[0].shape[1] // 2
    width = kx // slabs
    if width % LANES == 0:
        x_spec = pl.BlockSpec((rows, kx), functools.partial(lambda part, i, s: (0, part), part))
        part = 0
    else:
        x_spec = pl.BlockSpec((2 * slabs, rows, width), lambda i, s: (0, 0, 0))
    out = pl.BlockSpec((2 * rows, width), lambda i, s: (0, 0))
    return pl.pallas_call(
        functools.partial(sort_kernel, slabs, width, part, len(ties)),
        out_shape=[jax.ShapeDtypeStruct((2 * rows, width), jnp.bfloat16)] * (slabs // 2),
        grid_spec=pltpu.PrefetchScalarGridSpec(
            num_scalar_prefetch=1,
            grid=(1,),
            in_specs=[pl.BlockSpec(order.shape, lambda i, s: (0, 0, 0)), x_spec, x_spec] + [UNREAD] * len(ties),
            out_specs=[out] * (slabs // 2),
        ),
        compiler_params=params(width),
        cost_estimate=cost(3.0),
        name="sort_columns",
    )(me, order, *[far(by_slab(x, slabs, width)) for x in xs], *ties)


def swap(x, slabs, offset):
    return lax.ppermute(x, "slab", [(i, i ^ offset) for i in range(slabs)])


def exchange(pieces):
    return [pieces[0]] + [swap(pieces[i], 2 * len(pieces), 2 * i) for i in range(1, len(pieces))]


def volume_kernel(slabs, window, messages, first, ties, idx_ref, *refs):
    refs = refs[ties:]
    piece_refs, refs = refs[: slabs // 2], refs[slabs // 2 :]
    if first:
        sums_ref, meta_ref, code_refs = refs[0], refs[1], refs[2:-4]
    else:
        meta_ref, sums_ref, code_refs = refs[0], refs[1], refs[2:-4]
    all_ref, line_ref, scalar_ref, sem = refs[-4:]
    width = sums_ref.shape[3]
    rows = all_ref.shape[1]
    pick = (iota((16, LANES), 0) == iota((16, LANES), 1)).astype(jnp.bfloat16)
    for offset in range(slabs):
        if first:
            for i in range(rows // width):
                at = 2 * rows + 16 * (offset % 2 * (rows // width) + i)
                meta_ref[offset, :, i * width : (i + 1) * width] = piece_refs[offset // 2][at : at + 16, :]
        meta = meta_ref[offset]
        all_ref[offset] = lax.dot_general(
            meta, pick, (((0,), (0,)), ((), ())), preferred_element_type=jnp.float32
        ).astype(jnp.bfloat16)
        line_ref[offset : offset + 1, :] = meta.astype(jnp.float32)[10:11, 0:LANES].astype(jnp.int32) * ALIGN
    copy = pltpu.make_async_copy(line_ref, scalar_ref, sem)
    copy.start()
    copy.wait()

    def slab_sums(slab):
        about, here = [], []
        for offset in range(slabs):
            start = pl.multiple_of(scalar_ref[offset, slab], ALIGN)
            about.append(all_ref[offset, pl.ds(start, window), :])
            start = pl.multiple_of(offset % 2 * rows + start, ALIGN)
            here.append(piece_refs[offset // 2][pl.ds(start, window), :])
        about, here = jnp.concatenate(about, axis=0), jnp.concatenate(here, axis=0)
        meta = lax.dot_general(pick, about, (((1,), (1,)), ((), ())), preferred_element_type=jnp.float32)
        weights = meta[0:8]
        own = meta[8:9] == jnp.asarray(slab, jnp.float32)
        block = jnp.broadcast_to(jnp.where(own, meta[9:10], -1.0), weights.shape)
        spread = jnp.concatenate([jnp.where(block == float(b), weights, 0.0) for b in range(NBLK)], axis=0)
        sums = jnp.dot(spread.astype(jnp.bfloat16), here, preferred_element_type=jnp.float32)
        sums_ref[:, slab] = sums.reshape(YWIN, KZ_DEV, width)

    if slabs <= 8:
        for slab in range(slabs):
            slab_sums(slab)
    else:
        lax.fori_loop(0, slabs, lambda slab, carry: (slab_sums(slab), carry)[1], 0)
    portion = code_refs[0].shape[1] - ALIGN
    lines = portion // (slabs * KZ_DEV)
    at = 0
    for code_ref, count in zip(code_refs, messages):
        for i in range(count):
            x = sums_ref[pl.ds(idx_ref[at] * lines, lines)].reshape(portion, width)
            code_ref[i, :portion, :], code_ref[i, portion:, :] = encode(x)
            at += 1


def volume_sums(window, index, messages, groups, pieces, meta, ties):
    slabs = 2 * len(pieces)
    width = pieces[0].shape[1]
    first = meta is None
    rows = pieces[0].shape[0] // 2
    if first:
        rows = rows * width // (width + 16)
    portion = YWIN // groups * slabs * KZ_DEV
    out_shape = [
        jax.ShapeDtypeStruct((YWIN, slabs, KZ_DEV, width), jnp.float32),
    ]
    if first:
        out_shape.append(jax.ShapeDtypeStruct((slabs, 16, rows), jnp.bfloat16))
    out_shape += [jax.ShapeDtypeStruct((count, portion + ALIGN, width), jnp.int16) for count in messages]
    done = pl.pallas_call(
        functools.partial(volume_kernel, slabs, window, messages, first, len(ties)),
        out_shape=out_shape,
        in_specs=[SCALARS] + [UNREAD] * len(ties) + [WHOLE] * (len(pieces) + (0 if first else 1)),
        out_specs=[WHOLE] * len(out_shape),
        scratch_shapes=[
            pltpu.VMEM((slabs, rows, LANES), jnp.bfloat16),
            pltpu.VMEM((slabs, LANES), jnp.int32),
            pltpu.SMEM((slabs, LANES), jnp.int32),
            pltpu.SemaphoreType.DMA,
        ],
        compiler_params=params(width),
        cost_estimate=cost(7.0),
        name="volume_sums",
    )(index, *ties, *[far(x) for x in pieces], *([] if first else [meta]))
    sums = done[0].reshape(groups, portion, width)
    return (sums, done[2:], done[1]) if first else (sums, done[1:], meta)


def encode(x):
    rows, width = x.shape
    groups = rows // 8
    tiles = x.reshape(groups, 8, width)
    size = jnp.abs(tiles)
    most = jnp.max(jnp.max(size, axis=1), axis=1, keepdims=True)
    level = jnp.ceil(jnp.log2(jnp.maximum(most, 1e-30)) * STEPS) + 1.0
    inverse = jnp.broadcast_to(jnp.exp2(level * (-1.0 / STEPS)), (groups, width)).reshape(groups, 1, width)
    share = jnp.maximum(size * inverse, 1e-12)
    root = jnp.minimum(share * lax.rsqrt(share) * TOP + 0.5, TOP)
    code = jnp.where(tiles < 0, -root, root).reshape(rows, width).astype(jnp.int32).astype(jnp.int16)
    eye = iota((width, width), 0) == iota((width, width), 1)
    lines = [
        jnp.sum(jnp.where(eye, level[i * width : (i + 1) * width], 0.0), axis=0, keepdims=True)
        for i in range(groups // width)
    ]
    lines.append(jnp.zeros((ALIGN - len(lines), width), jnp.float32))
    return code, jnp.concatenate(lines, axis=0).astype(jnp.int32).astype(jnp.int16)


def decode(code, lines):
    rows, width = code.shape
    groups = rows // 8
    x = code.astype(jnp.int32).astype(jnp.float32)
    lines = lines.astype(jnp.int32).astype(jnp.float32)
    eye = iota((width, width), 0) == iota((width, width), 1)
    level = jnp.concatenate(
        [jnp.sum(jnp.where(eye, lines[i : i + 1], 0.0), axis=1, keepdims=True) for i in range(groups // width)],
        axis=0,
    )
    scale = jnp.exp2(level * (1.0 / STEPS)) * (1.0 / (TOP * TOP))
    scale = jnp.broadcast_to(scale, (groups, width)).reshape(groups, 1, width)
    return ((x * jnp.abs(x)).reshape(groups, 8, width) * scale).reshape(rows, width)


def hop_kernel(places, idx_ref, sums_ref, prev_ref, *refs):
    out_ref = refs[-1]
    rows = sums_ref.shape[1]
    for i, place in enumerate(places):
        x = sums_ref[idx_ref[i]] + decode(prev_ref[place, :rows, :], prev_ref[place, rows:, :])
        out_ref[i, :rows, :], out_ref[i, rows:, :] = encode(x)


def hop(index, sums, prev, places, ties):
    _, rows, width = sums.shape
    count = len(places)
    return pl.pallas_call(
        functools.partial(hop_kernel, places),
        out_shape=jax.ShapeDtypeStruct((count, rows + ALIGN, width), jnp.int16),
        in_specs=[SCALARS, WHOLE, WHOLE] + [UNREAD] * len(ties),
        out_specs=WHOLE,
        compiler_params=params(width),
        cost_estimate=cost(2.0 + count),
        name="hop",
    )(index, sums, prev, *ties)


def portions(z, groups, r):
    return jnp.where(z >= groups // 2, groups - 1 - r, r).astype(jnp.int32)


class AlongZ:
    def __init__(self, sums, first, payloads, z, groups):
        self.sums, self.z, self.groups, self.ends = sums, z, groups, []
        half = groups // 2
        got = [{r: self.send(x, [(0, 1)]) for r, x in zip(first, payloads)}]
        hops = []
        for k in range(2, half):
            got.append({})
            for r in range(groups - 1, k, -1):
                hops.append(functools.partial(self.move, got[k - 2], r, got[k - 1], r, [(k - 1, k)]))
        across = {}
        for r in range(groups - 1, half - 1, -1):
            hops.append(functools.partial(self.move, got[half - 2], r, across, groups - 1 - r, [(half - 1, half)]))
        outward = across
        for j in range(half - 1, 1, -1):
            kept, new = {}, {}
            hops.append(functools.partial(self.move, got[j - 2], j, kept, j, [(j - 1, j)], True))
            for r in range(j):
                hops.append(functools.partial(self.move, outward, r, new, r, [(j, j - 1)], r == j - 1))
            outward = new
        hops.append(functools.partial(self.move, outward, 0, {}, 0, [(1, 0), (0, 1)], True, True))
        self.hops, self.keep = hops, half - 1

    def send(self, payload, pairs):
        last = self.groups - 1
        return lax.ppermute(payload, "grp", pairs + [(last - a, last - b) for a, b in pairs])

    def move(self, source, r, target, place, pairs, final=False, both=False, ties=()):
        last = self.groups - 1
        wanted = jnp.full((1,), r, jnp.int32)
        if both:
            wanted = jnp.where(jnp.minimum(self.z, last - self.z) == 0, 1, 0).astype(jnp.int32).reshape(1)
        payload = hop(portions(self.z, self.groups, wanted), self.sums, source[r], [0], ties)
        target[place] = self.send(payload, pairs)
        if final or (len(pairs) == 1 and pairs[0] == (self.keep, self.keep + 1) and place == self.keep):
            self.ends.append((target[place], 0))
        return payload


def image_kernel(parts, zs, own_ref, *refs):
    tau_ref, high_ref, low_ref, out_ref = refs[-4:]
    each = len(refs[:-4]) // 3
    volume = []
    for c in range(3):
        sums_ref, coded = refs[c * each], refs[c * each + 1 : (c + 1) * each]
        rows = sums_ref.shape[1]
        x = sums_ref[0]
        for ref in coded:
            x = x + decode(ref[0, :rows, :], ref[0, rows:, :])
        volume.append(x)
    below = volume[2] + tau_ref[...]
    columns = []
    for c in range(2):
        x = volume[c] / below
        columns += [x[k * zs : (k + 1) * zs] for k in range(parts)]
    x = jnp.concatenate(columns, axis=1)
    x_high = x.astype(jnp.bfloat16)
    x_low = (x - x_high.astype(jnp.float32)).astype(jnp.bfloat16)
    dot = functools.partial(jnp.dot, preferred_element_type=jnp.float32)
    y = dot(high_ref[...], x_high) + (dot(high_ref[...], x_low) + dot(low_ref[...], x_high))
    span = x.shape[1] // 2
    width = span // parts
    real = y[:zs, :span] - y[zs:, span:]
    imag = y[zs:, :span] + y[:zs, span:]
    for k in range(parts):
        out_ref[0, k] = real[:, k * width : (k + 1) * width]
        out_ref[1, k] = imag[:, k * width : (k + 1) * width]


def image_of(own, fields, tau, zs):
    rows, width = fields[0][0].shape[1:]
    parts = rows // zs
    operands, specs = [], []
    for sums, ends in fields:
        operands.append(sums)
        specs.append(pl.BlockSpec((1, rows, width), lambda i, s: (s[0], 0, 0)))
        for payload, place in ends:
            operands.append(payload)
            specs.append(pl.BlockSpec((1, rows + ALIGN, width), functools.partial(lambda place, i, s: (place, 0, 0), place)))
    steps = np.arange(zs)
    angles = (steps[:, None] * steps[None, :] % zs) * (2.0 * math.pi / zs)
    table = (np.concatenate([np.cos(angles), np.sin(angles)], axis=0) / math.sqrt(zs)).astype(np.float32)
    high = table.astype(jnp.bfloat16)
    low = (table - high.astype(np.float32)).astype(jnp.bfloat16)
    for x in (tau.reshape(1, width), jnp.asarray(high), jnp.asarray(low)):
        operands.append(x)
        specs.append(pl.BlockSpec(x.shape, lambda i, s: (0, 0)))
    return pl.pallas_call(
        functools.partial(image_kernel, parts, zs),
        out_shape=jax.ShapeDtypeStruct((2, parts, zs, width), jnp.float32),
        grid_spec=pltpu.PrefetchScalarGridSpec(
            num_scalar_prefetch=1,
            grid=(1,),
            in_specs=specs,
            out_specs=pl.BlockSpec((2, parts, zs, width), lambda i, s: (0, 0, 0, 0)),
        ),
        compiler_params=params(width),
        cost_estimate=cost(6.0),
        name="image_of",
    )(own, *[far(x) for x in operands])


def on_device(spectra, ctf_sq, dest, block, pattern, pattern_table, tau):
    slabs, groups = lax.axis_size("slab"), lax.axis_size("grp")
    rows, kx = ctf_sq.shape
    capacity = max(2, 2 * rows // slabs)
    window = min(rows, -(-capacity // ALIGN) * ALIGN + ALIGN)
    width = kx // slabs
    slab, z = lax.axis_index("slab"), lax.axis_index("grp")
    me = slab.astype(jnp.int32).reshape(1)
    ids = jnp.stack([dest[:, 0], block, pattern])
    ids, ctf_sq, spectra = [(x, swap(x, slabs, 1)) for x in (ids, ctf_sq, spectra)]
    order, ctf = plan_rows(slabs, window, me, ids, pattern_table, ctf_sq)
    first = list(range(groups - 1, 1, -1))
    index = portions(z, groups, np.array(first))

    def volume(piece, meta, ties):
        sums, payloads, meta = volume_sums(window, index, [1] * len(first), groups, piece, meta, ties)
        return AlongZ(sums, first, payloads, z, groups), payloads[0], meta

    real = sort_columns(slabs, me, order, spectra, 0, ())
    ctf, real_there = exchange(ctf), exchange(real)
    imag = sort_columns(slabs, me, order, spectra, 1, (real[0],))
    ctf_part, coded, meta = volume(ctf, None, (imag[0],))
    imag_there = exchange(imag)
    real_part, coded, _ = volume(real_there, meta, (coded,))
    tie = coded
    early = len(ctf_part.hops) - 1
    for step in ctf_part.hops[:early]:
        tie = step(ties=(tie,))
    imag_part, coded, _ = volume(imag_there, meta, (tie,))
    steps = real_part.hops[:-1] + imag_part.hops[:1] + ctf_part.hops[early:] + real_part.hops[-1:] + imag_part.hops[1:]
    tie = coded
    for step in steps:
        tie = step(ties=(tie,))
    fields = [(part.sums, part.ends) for part in (ctf_part, real_part, imag_part)]
    tau_here = lax.dynamic_slice_in_dim(tau, slab * width, width, 0)
    own = z.astype(jnp.int32).reshape(1)
    return image_of(own, [fields[1], fields[2], fields[0]], tau_here, KZ_DEV * slabs)


def solution(mesh):
    in_specs = (
        P(("grp", "slab"), None),
        P(("grp", "slab"), None),
        P(("grp", "slab"), None),
        P(("grp", "slab")),
        P(("grp", "slab")),
        P(),
        P(),
    )
    out_specs = P(None, "grp", None, "slab")
    return jax.shard_map(
        on_device, mesh=mesh, in_specs=in_specs, out_specs=out_specs, check_vma=False
    )
```

```python
import functools
import math

import jax
import jax.numpy as jnp
import numpy as np
from jax import lax
from jax.experimental import pallas as pl
from jax.experimental.pallas import tpu as pltpu
from jax.sharding import PartitionSpec as P

KZ_DEV = 32
YWIN = 16
NBLK = 64
LANES = 128
ALIGN = 16
TOP = 32767.0
STEPS = 256.0
VMEM = 60 * 1024 * 1024

WHOLE = pl.BlockSpec(memory_space=pltpu.VMEM)
SCALARS = pl.BlockSpec(memory_space=pltpu.SMEM)
UNREAD = pl.BlockSpec(memory_space=pl.ANY)


def params(width):
    return pltpu.CompilerParams(vmem_limit_bytes=VMEM if width < LANES else VMEM // 2)


def far(x):
    return pltpu.with_memory_space_constraint(x, pltpu.HBM)


def cost(micros):
    return pl.CostEstimate(flops=0, bytes_accessed=int(micros * 3.0e6), transcendentals=0)


def iota(shape, axis):
    return lax.broadcasted_iota(jnp.int32, shape, axis)


def plan(slabs, window, dest, block, pattern, table):
    rows = dest.shape[1]
    mine = (dest == iota((slabs, rows), 0)).astype(jnp.float32)
    before = (iota((rows, rows), 0) < iota((rows, rows), 1)).astype(jnp.bfloat16)
    rank = jnp.dot(mine.astype(jnp.bfloat16), before, preferred_element_type=jnp.float32)
    counts = jnp.sum(mine, axis=1, keepdims=True)
    slab_of = iota((slabs, rows), 0)
    first = jnp.sum(jnp.where(slab_of < dest, counts, 0.0), axis=0, keepdims=True)
    target = (first + jnp.sum(mine * rank, axis=0, keepdims=True)).astype(jnp.int32)
    order = (target == iota((rows, rows), 0)).astype(jnp.bfloat16)
    ids = (pattern == iota((table.shape[1], rows), 0)).astype(jnp.bfloat16)
    weights = jnp.dot(table, ids, preferred_element_type=jnp.float32)
    line = iota((8, rows), 0)
    named = jnp.where(line == 0, dest, jnp.where(line == 1, block, 0)).astype(jnp.float32)
    given = jnp.concatenate([weights, named], axis=0).astype(jnp.bfloat16)
    ordered = lax.dot_general(given, order, (((1,), (1,)), ((), ())), preferred_element_type=jnp.float32)
    start = jnp.sum(jnp.where(slab_of < iota((slabs, rows), 1), counts, 0.0), axis=0, keepdims=True)
    start = jnp.minimum(start.astype(jnp.int32) // ALIGN, (rows - window) // ALIGN).astype(jnp.float32)
    meta = jnp.where(iota((16, rows), 0) == 10, start, ordered).astype(jnp.bfloat16)
    return order, meta


def piece_of(x_ref, column, width):
    if len(x_ref.shape) == 3:
        return x_ref[column]
    return x_ref[:, pl.ds(pl.multiple_of(column * width, width), width)]


def by_slab(x, slabs, width):
    if width % LANES == 0:
        return x
    return x.reshape(x.shape[0], -1, width).transpose(1, 0, 2)


def sorted_piece(order, x_ref, column, width):
    piece = piece_of(x_ref, column, width)
    return jnp.dot(order, piece, preferred_element_type=jnp.float32).astype(jnp.bfloat16)


def plan_kernel(slabs, window, width, me_ref, *refs):
    ids_refs, table_ref, x_refs, order_ref, out_refs = refs[0:2], refs[2], refs[3:5], refs[5], refs[6:]
    rows = order_ref.shape[1]
    lines = 16 * (rows // width)
    for half in range(2):
        ids = ids_refs[half][...]
        order, meta = plan(slabs, window, ids[0:1], ids[1:2], ids[2:3], table_ref[...])
        order_ref[half] = order
        for i, out in enumerate(out_refs):
            column = jnp.bitwise_xor(me_ref[0], 2 * i)
            out[half * rows : (half + 1) * rows, :] = sorted_piece(order, x_refs[half], column, width)
            for j in range(rows // width):
                at = 2 * rows + half * lines + 16 * j
                out[at : at + 16, :] = meta[:, j * width : (j + 1) * width]


def plan_rows(slabs, window, me, ids, table, xs):
    rows, kx = xs[0].shape
    width = kx // slabs
    out = jax.ShapeDtypeStruct((2 * rows + 32 * (rows // width), width), jnp.bfloat16)
    done = pl.pallas_call(
        functools.partial(plan_kernel, slabs, window, width),
        out_shape=[jax.ShapeDtypeStruct((2, rows, rows), jnp.bfloat16)] + [out] * (slabs // 2),
        in_specs=[SCALARS] + [WHOLE] * 5,
        out_specs=[WHOLE] * (1 + slabs // 2),
        compiler_params=params(width),
        cost_estimate=cost(6.0),
        name="plan_rows",
    )(me, far(ids[0]), ids[1], far(table.T), far(by_slab(xs[0], slabs, width)), by_slab(xs[1], slabs, width))
    return done[0], done[1:]


def sort_kernel(slabs, width, part, ties, me_ref, order_ref, *refs):
    x_refs, out_refs = refs[0:2], refs[2 + ties :]
    rows = order_ref.shape[1]
    for i, out in enumerate(out_refs):
        column = jnp.bitwise_xor(me_ref[0], 2 * i) + part * slabs
        for half in range(2):
            out[half * rows : (half + 1) * rows, :] = sorted_piece(order_ref[half], x_refs[half], column, width)


def sort_columns(slabs, me, order, xs, part, ties):
    rows, kx = order.shape[1], xs[0].shape[1] // 2
    width = kx // slabs
    if width % LANES == 0:
        x_spec = pl.BlockSpec((rows, kx), functools.partial(lambda part, i, s: (0, part), part))
        part = 0
    else:
        x_spec = pl.BlockSpec((2 * slabs, rows, width), lambda i, s: (0, 0, 0))
    out = pl.BlockSpec((2 * rows, width), lambda i, s: (0, 0))
    return pl.pallas_call(
        functools.partial(sort_kernel, slabs, width, part, len(ties)),
        out_shape=[jax.ShapeDtypeStruct((2 * rows, width), jnp.bfloat16)] * (slabs // 2),
        grid_spec=pltpu.PrefetchScalarGridSpec(
            num_scalar_prefetch=1,
            grid=(1,),
            in_specs=[pl.BlockSpec(order.shape, lambda i, s: (0, 0, 0)), x_spec, x_spec] + [UNREAD] * len(ties),
            out_specs=[out] * (slabs // 2),
        ),
        compiler_params=params(width),
        cost_estimate=cost(3.0),
        name="sort_columns",
    )(me, order, *[far(by_slab(x, slabs, width)) for x in xs], *ties)


def swap(x, slabs, offset):
    return lax.ppermute(x, "slab", [(i, i ^ offset) for i in range(slabs)])


def exchange(pieces):
    return [pieces[0]] + [swap(pieces[i], 2 * len(pieces), 2 * i) for i in range(1, len(pieces))]


def volume_kernel(slabs, window, messages, first, ties, idx_ref, *refs):
    refs = refs[ties:]
    piece_refs, refs = refs[: slabs // 2], refs[slabs // 2 :]
    if first:
        sums_ref, meta_ref, code_refs = refs[0], refs[1], refs[2:-4]
    else:
        meta_ref, sums_ref, code_refs = refs[0], refs[1], refs[2:-4]
    all_ref, line_ref, scalar_ref, sem = refs[-4:]
    width = sums_ref.shape[3]
    rows = all_ref.shape[1]
    pick = (iota((16, LANES), 0) == iota((16, LANES), 1)).astype(jnp.bfloat16)
    for offset in range(slabs):
        if first:
            for i in range(rows // width):
                at = 2 * rows + 16 * (offset % 2 * (rows // width) + i)
                meta_ref[offset, :, i * width : (i + 1) * width] = piece_refs[offset // 2][at : at + 16, :]
        meta = meta_ref[offset]
        all_ref[offset] = lax.dot_general(
            meta, pick, (((0,), (0,)), ((), ())), preferred_element_type=jnp.float32
        ).astype(jnp.bfloat16)
        line_ref[offset : offset + 1, :] = meta.astype(jnp.float32)[10:11, 0:LANES].astype(jnp.int32) * ALIGN
    copy = pltpu.make_async_copy(line_ref, scalar_ref, sem)
    copy.start()
    copy.wait()

    def slab_sums(slab):
        about, here = [], []
        for offset in range(slabs):
            start = pl.multiple_of(scalar_ref[offset, slab], ALIGN)
            about.append(all_ref[offset, pl.ds(start, window), :])
            start = pl.multiple_of(offset % 2 * rows + start, ALIGN)
            here.append(piece_refs[offset // 2][pl.ds(start, window), :])
        about, here = jnp.concatenate(about, axis=0), jnp.concatenate(here, axis=0)
        meta = lax.dot_general(pick, about, (((1,), (1,)), ((), ())), preferred_element_type=jnp.float32)
        weights = meta[0:8]
        own = meta[8:9] == jnp.asarray(slab, jnp.float32)
        block = jnp.broadcast_to(jnp.where(own, meta[9:10], -1.0), weights.shape)
        spread = jnp.concatenate([jnp.where(block == float(b), weights, 0.0) for b in range(NBLK)], axis=0)
        sums = jnp.dot(spread.astype(jnp.bfloat16), here, preferred_element_type=jnp.float32)
        sums_ref[:, slab] = sums.reshape(YWIN, KZ_DEV, width)

    if slabs <= 8:
        for slab in range(slabs):
            slab_sums(slab)
    else:
        lax.fori_loop(0, slabs, lambda slab, carry: (slab_sums(slab), carry)[1], 0)
    portion = code_refs[0].shape[1] - ALIGN
    lines = portion // (slabs * KZ_DEV)
    at = 0
    for code_ref, count in zip(code_refs, messages):
        for i in range(count):
            x = sums_ref[pl.ds(idx_ref[at] * lines, lines)].reshape(portion, width)
            code_ref[i, :portion, :], code_ref[i, portion:, :] = encode(x)
            at += 1


def volume_sums(window, index, messages, groups, pieces, meta, ties):
    slabs = 2 * len(pieces)
    width = pieces[0].shape[1]
    first = meta is None
    rows = pieces[0].shape[0] // 2
    if first:
        rows = rows * width // (width + 16)
    portion = YWIN // groups * slabs * KZ_DEV
    out_shape = [
        jax.ShapeDtypeStruct((YWIN, slabs, KZ_DEV, width), jnp.float32),
    ]
    if first:
        out_shape.append(jax.ShapeDtypeStruct((slabs, 16, rows), jnp.bfloat16))
    out_shape += [jax.ShapeDtypeStruct((count, portion + ALIGN, width), jnp.int16) for count in messages]
    done = pl.pallas_call(
        functools.partial(volume_kernel, slabs, window, messages, first, len(ties)),
        out_shape=out_shape,
        in_specs=[SCALARS] + [UNREAD] * len(ties) + [WHOLE] * (len(pieces) + (0 if first else 1)),
        out_specs=[WHOLE] * len(out_shape),
        scratch_shapes=[
            pltpu.VMEM((slabs, rows, LANES), jnp.bfloat16),
            pltpu.VMEM((slabs, LANES), jnp.int32),
            pltpu.SMEM((slabs, LANES), jnp.int32),
            pltpu.SemaphoreType.DMA,
        ],
        compiler_params=params(width),
        cost_estimate=cost(7.0),
        name="volume_sums",
    )(index, *ties, *[far(x) for x in pieces], *([] if first else [meta]))
    sums = done[0].reshape(groups, portion, width)
    return (sums, done[2:], done[1]) if first else (sums, done[1:], meta)


def encode(x):
    rows, width = x.shape
    groups = rows // 8
    tiles = x.reshape(groups, 8, width)
    size = jnp.abs(tiles)
    most = jnp.max(jnp.max(size, axis=1), axis=1, keepdims=True)
    level = jnp.ceil(jnp.log2(jnp.maximum(most, 1e-30)) * STEPS) + 1.0
    inverse = jnp.broadcast_to(jnp.exp2(level * (-1.0 / STEPS)), (groups, width)).reshape(groups, 1, width)
    share = jnp.maximum(size * inverse, 1e-12)
    root = jnp.minimum(share * lax.rsqrt(share) * TOP + 0.5, TOP)
    code = jnp.where(tiles < 0, -root, root).reshape(rows, width).astype(jnp.int32).astype(jnp.int16)
    eye = iota((width, width), 0) == iota((width, width), 1)
    lines = [
        jnp.sum(jnp.where(eye, level[i * width : (i + 1) * width], 0.0), axis=0, keepdims=True)
        for i in range(groups // width)
    ]
    lines.append(jnp.zeros((ALIGN - len(lines), width), jnp.float32))
    return code, jnp.concatenate(lines, axis=0).astype(jnp.int32).astype(jnp.int16)


def decode(code, lines):
    rows, width = code.shape
    groups = rows // 8
    x = code.astype(jnp.int32).astype(jnp.float32)
    lines = lines.astype(jnp.int32).astype(jnp.float32)
    eye = iota((width, width), 0) == iota((width, width), 1)
    level = jnp.concatenate(
        [jnp.sum(jnp.where(eye, lines[i : i + 1], 0.0), axis=1, keepdims=True) for i in range(groups // width)],
        axis=0,
    )
    scale = jnp.exp2(level * (1.0 / STEPS)) * (1.0 / (TOP * TOP))
    scale = jnp.broadcast_to(scale, (groups, width)).reshape(groups, 1, width)
    return ((x * jnp.abs(x)).reshape(groups, 8, width) * scale).reshape(rows, width)


def hop_kernel(places, idx_ref, sums_ref, prev_ref, *refs):
    out_ref = refs[-1]
    rows = sums_ref.shape[1]
    for i, place in enumerate(places):
        x = sums_ref[idx_ref[i]] + decode(prev_ref[place, :rows, :], prev_ref[place, rows:, :])
        out_ref[i, :rows, :], out_ref[i, rows:, :] = encode(x)


def hop(index, sums, prev, places, ties):
    _, rows, width = sums.shape
    count = len(places)
    return pl.pallas_call(
        functools.partial(hop_kernel, places),
        out_shape=jax.ShapeDtypeStruct((count, rows + ALIGN, width), jnp.int16),
        in_specs=[SCALARS, WHOLE, WHOLE] + [UNREAD] * len(ties),
        out_specs=WHOLE,
        compiler_params=params(width),
        cost_estimate=cost(2.0 + count),
        name="hop",
    )(index, sums, prev, *ties)


def portions(z, groups, r):
    return jnp.where(z >= groups // 2, groups - 1 - r, r).astype(jnp.int32)


class AlongZ:
    def __init__(self, sums, first, payloads, z, groups):
        self.sums, self.z, self.groups, self.ends = sums, z, groups, []
        half = groups // 2
        got = [{r: self.send(x, [(0, 1)]) for r, x in zip(first, payloads)}]
        hops = []
        for k in range(2, half):
            got.append({})
            for r in range(groups - 1, k, -1):
                hops.append(functools.partial(self.move, got[k - 2], r, got[k - 1], r, [(k - 1, k)]))
        across = {}
        for r in range(groups - 1, half - 1, -1):
            hops.append(functools.partial(self.move, got[half - 2], r, across, groups - 1 - r, [(half - 1, half)]))
        outward = across
        for j in range(half - 1, 1, -1):
            kept, new = {}, {}
            hops.append(functools.partial(self.move, got[j - 2], j, kept, j, [(j - 1, j)], True))
            for r in range(j):
                hops.append(functools.partial(self.move, outward, r, new, r, [(j, j - 1)], r == j - 1))
            outward = new
        hops.append(functools.partial(self.move, outward, 0, {}, 0, [(1, 0), (0, 1)], True, True))
        self.hops, self.keep = hops, half - 1

    def send(self, payload, pairs):
        last = self.groups - 1
        return lax.ppermute(payload, "grp", pairs + [(last - a, last - b) for a, b in pairs])

    def move(self, source, r, target, place, pairs, final=False, both=False, ties=()):
        last = self.groups - 1
        wanted = jnp.full((1,), r, jnp.int32)
        if both:
            wanted = jnp.where(jnp.minimum(self.z, last - self.z) == 0, 1, 0).astype(jnp.int32).reshape(1)
        payload = hop(portions(self.z, self.groups, wanted), self.sums, source[r], [0], ties)
        target[place] = self.send(payload, pairs)
        if final or (len(pairs) == 1 and pairs[0] == (self.keep, self.keep + 1) and place == self.keep):
            self.ends.append((target[place], 0))
        return payload


def image_kernel(parts, zs, own_ref, *refs):
    tau_ref, high_ref, low_ref, out_ref = refs[-4:]
    each = len(refs[:-4]) // 3
    volume = []
    for c in range(3):
        sums_ref, coded = refs[c * each], refs[c * each + 1 : (c + 1) * each]
        rows = sums_ref.shape[1]
        x = sums_ref[0]
        for ref in coded:
            x = x + decode(ref[0, :rows, :], ref[0, rows:, :])
        volume.append(x)
    below = volume[2] + tau_ref[...]
    columns = []
    for c in range(2):
        x = volume[c] / below
        columns += [x[k * zs : (k + 1) * zs] for k in range(parts)]
    x = jnp.concatenate(columns, axis=1)
    x_high = x.astype(jnp.bfloat16)
    x_low = (x - x_high.astype(jnp.float32)).astype(jnp.bfloat16)
    dot = functools.partial(jnp.dot, preferred_element_type=jnp.float32)
    y = dot(high_ref[...], x_high) + (dot(high_ref[...], x_low) + dot(low_ref[...], x_high))
    span = x.shape[1] // 2
    width = span // parts
    real = y[:zs, :span] - y[zs:, span:]
    imag = y[zs:, :span] + y[:zs, span:]
    for k in range(parts):
        out_ref[0, k] = real[:, k * width : (k + 1) * width]
        out_ref[1, k] = imag[:, k * width : (k + 1) * width]


def image_of(own, fields, tau, zs):
    rows, width = fields[0][0].shape[1:]
    parts = rows // zs
    operands, specs = [], []
    for sums, ends in fields:
        operands.append(sums)
        specs.append(pl.BlockSpec((1, rows, width), lambda i, s: (s[0], 0, 0)))
        for payload, place in ends:
            operands.append(payload)
            specs.append(pl.BlockSpec((1, rows + ALIGN, width), functools.partial(lambda place, i, s: (place, 0, 0), place)))
    steps = np.arange(zs)
    angles = (steps[:, None] * steps[None, :] % zs) * (2.0 * math.pi / zs)
    table = (np.concatenate([np.cos(angles), np.sin(angles)], axis=0) / math.sqrt(zs)).astype(np.float32)
    high = table.astype(jnp.bfloat16)
    low = (table - high.astype(np.float32)).astype(jnp.bfloat16)
    for x in (tau.reshape(1, width), jnp.asarray(high), jnp.asarray(low)):
        operands.append(x)
        specs.append(pl.BlockSpec(x.shape, lambda i, s: (0, 0)))
    return pl.pallas_call(
        functools.partial(image_kernel, parts, zs),
        out_shape=jax.ShapeDtypeStruct((2, parts, zs, width), jnp.float32),
        grid_spec=pltpu.PrefetchScalarGridSpec(
            num_scalar_prefetch=1,
            grid=(1,),
            in_specs=specs,
            out_specs=pl.BlockSpec((2, parts, zs, width), lambda i, s: (0, 0, 0, 0)),
        ),
        compiler_params=params(width),
        cost_estimate=cost(6.0),
        name="image_of",
    )(own, *[far(x) for x in operands])


def on_device(spectra, ctf_sq, dest, block, pattern, pattern_table, tau):
    slabs, groups = lax.axis_size("slab"), lax.axis_size("grp")
    rows, kx = ctf_sq.shape
    capacity = max(2, 2 * rows // slabs)
    window = min(rows, -(-capacity // ALIGN) * ALIGN + ALIGN)
    width = kx // slabs
    slab, z = lax.axis_index("slab"), lax.axis_index("grp")
    me = slab.astype(jnp.int32).reshape(1)
    ids = jnp.stack([dest[:, 0], block, pattern])
    ids, ctf_sq, spectra = [(x, swap(x, slabs, 1)) for x in (ids, ctf_sq, spectra)]
    order, ctf = plan_rows(slabs, window, me, ids, pattern_table, ctf_sq)
    first = list(range(groups - 1, 1, -1))
    index = portions(z, groups, np.array(first))

    def volume(piece, meta, ties):
        sums, payloads, meta = volume_sums(window, index, [1] * len(first), groups, piece, meta, ties)
        return AlongZ(sums, first, payloads, z, groups), payloads[0], meta

    real = sort_columns(slabs, me, order, spectra, 0, ())
    ctf, real_there = exchange(ctf), exchange(real)
    imag = sort_columns(slabs, me, order, spectra, 1, (real[0],))
    ctf_part, coded, meta = volume(ctf, None, (imag[0],))
    imag_there = exchange(imag)
    real_part, coded, _ = volume(real_there, meta, (coded,))
    tie = coded
    early = len(ctf_part.hops) - 1
    for step in ctf_part.hops[:early]:
        tie = step(ties=(tie,))
    imag_part, coded, _ = volume(imag_there, meta, (tie,))
    left = imag_part.hops[1:]
    if groups == 4:
        left = left[::-1]
    steps = real_part.hops[:-1] + imag_part.hops[:1] + ctf_part.hops[early:] + real_part.hops[-1:] + left
    tie = coded
    for step in steps:
        tie = step(ties=(tie,))
    fields = [(part.sums, part.ends) for part in (ctf_part, real_part, imag_part)]
    tau_here = lax.dynamic_slice_in_dim(tau, slab * width, width, 0)
    own = z.astype(jnp.int32).reshape(1)
    return image_of(own, [fields[1], fields[2], fields[0]], tau_here, KZ_DEV * slabs)


def solution(mesh):
    in_specs = (
        P(("grp", "slab"), None),
        P(("grp", "slab"), None),
        P(("grp", "slab"), None),
        P(("grp", "slab")),
        P(("grp", "slab")),
        P(),
        P(),
    )
    out_specs = P(None, "grp", None, "slab")
    return jax.shard_map(
        on_device, mesh=mesh, in_specs=in_specs, out_specs=out_specs, check_vma=False
    )
```

```python
import functools
import math

import jax
import jax.numpy as jnp
import numpy as np
from jax import lax
from jax.experimental import pallas as pl
from jax.experimental.pallas import tpu as pltpu
from jax.sharding import PartitionSpec as P

KZ_DEV = 32
YWIN = 16
NBLK = 64
LANES = 128
ALIGN = 16
TOP = 32767.0
STEPS = 256.0
VMEM = 60 * 1024 * 1024

WHOLE = pl.BlockSpec(memory_space=pltpu.VMEM)
SCALARS = pl.BlockSpec(memory_space=pltpu.SMEM)
UNREAD = pl.BlockSpec(memory_space=pl.ANY)


def params(width):
    return pltpu.CompilerParams(vmem_limit_bytes=VMEM if width < LANES else VMEM // 2)


def far(x):
    return pltpu.with_memory_space_constraint(x, pltpu.HBM)


def cost(micros):
    return pl.CostEstimate(flops=0, bytes_accessed=int(micros * 3.0e6), transcendentals=0)


def iota(shape, axis):
    return lax.broadcasted_iota(jnp.int32, shape, axis)


def plan(slabs, window, dest, block, pattern, table):
    rows = dest.shape[1]
    mine = (dest == iota((slabs, rows), 0)).astype(jnp.float32)
    before = (iota((rows, rows), 0) < iota((rows, rows), 1)).astype(jnp.bfloat16)
    rank = jnp.dot(mine.astype(jnp.bfloat16), before, preferred_element_type=jnp.float32)
    counts = jnp.sum(mine, axis=1, keepdims=True)
    slab_of = iota((slabs, rows), 0)
    first = jnp.sum(jnp.where(slab_of < dest, counts, 0.0), axis=0, keepdims=True)
    target = (first + jnp.sum(mine * rank, axis=0, keepdims=True)).astype(jnp.int32)
    order = (target == iota((rows, rows), 0)).astype(jnp.bfloat16)
    ids = (pattern == iota((table.shape[1], rows), 0)).astype(jnp.bfloat16)
    weights = jnp.dot(table, ids, preferred_element_type=jnp.float32)
    line = iota((8, rows), 0)
    named = jnp.where(line == 0, dest, jnp.where(line == 1, block, 0)).astype(jnp.float32)
    given = jnp.concatenate([weights, named], axis=0).astype(jnp.bfloat16)
    ordered = lax.dot_general(given, order, (((1,), (1,)), ((), ())), preferred_element_type=jnp.float32)
    start = jnp.sum(jnp.where(slab_of < iota((slabs, rows), 1), counts, 0.0), axis=0, keepdims=True)
    start = jnp.minimum(start.astype(jnp.int32) // ALIGN, (rows - window) // ALIGN).astype(jnp.float32)
    meta = jnp.where(iota((16, rows), 0) == 10, start, ordered).astype(jnp.bfloat16)
    return order, meta


def piece_of(x_ref, column, width):
    if len(x_ref.shape) == 3:
        return x_ref[column]
    return x_ref[:, pl.ds(pl.multiple_of(column * width, width), width)]


def by_slab(x, slabs, width):
    if width % LANES == 0:
        return x
    return x.reshape(x.shape[0], -1, width).transpose(1, 0, 2)


def sorted_piece(order, x_ref, column, width):
    piece = piece_of(x_ref, column, width)
    return jnp.dot(order, piece, preferred_element_type=jnp.float32).astype(jnp.bfloat16)


def plan_kernel(slabs, window, width, me_ref, *refs):
    ids_refs, table_ref, x_refs, order_ref, out_refs = refs[0:2], refs[2], refs[3:5], refs[5], refs[6:]
    rows = order_ref.shape[1]
    lines = 16 * (rows // width)
    for half in range(2):
        ids = ids_refs[half][...]
        order, meta = plan(slabs, window, ids[0:1], ids[1:2], ids[2:3], table_ref[...])
        order_ref[half] = order
        for i, out in enumerate(out_refs):
            column = jnp.bitwise_xor(me_ref[0], 2 * i)
            out[half * rows : (half + 1) * rows, :] = sorted_piece(order, x_refs[half], column, width)
            for j in range(rows // width):
                at = 2 * rows + half * lines + 16 * j
                out[at : at + 16, :] = meta[:, j * width : (j + 1) * width]


def plan_rows(slabs, window, me, ids, table, xs):
    rows, kx = xs[0].shape
    width = kx // slabs
    out = jax.ShapeDtypeStruct((2 * rows + 32 * (rows // width), width), jnp.bfloat16)
    done = pl.pallas_call(
        functools.partial(plan_kernel, slabs, window, width),
        out_shape=[jax.ShapeDtypeStruct((2, rows, rows), jnp.bfloat16)] + [out] * (slabs // 2),
        in_specs=[SCALARS] + [WHOLE] * 5,
        out_specs=[WHOLE] * (1 + slabs // 2),
        compiler_params=params(width),
        cost_estimate=cost(6.0),
        name="plan_rows",
    )(me, far(ids[0]), ids[1], far(table.T), far(by_slab(xs[0], slabs, width)), by_slab(xs[1], slabs, width))
    return done[0], done[1:]


def sort_kernel(slabs, width, part, ties, me_ref, order_ref, *refs):
    x_refs, out_refs = refs[0:2], refs[2 + ties :]
    rows = order_ref.shape[1]
    for i, out in enumerate(out_refs):
        column = jnp.bitwise_xor(me_ref[0], 2 * i) + part * slabs
        for half in range(2):
            out[half * rows : (half + 1) * rows, :] = sorted_piece(order_ref[half], x_refs[half], column, width)


def sort_columns(slabs, me, order, xs, part, ties):
    rows, kx = order.shape[1], xs[0].shape[1] // 2
    width = kx // slabs
    if width % LANES == 0:
        x_spec = pl.BlockSpec((rows, kx), functools.partial(lambda part, i, s: (0, part), part))
        part = 0
    else:
        x_spec = pl.BlockSpec((2 * slabs, rows, width), lambda i, s: (0, 0, 0))
    out = pl.BlockSpec((2 * rows, width), lambda i, s: (0, 0))
    return pl.pallas_call(
        functools.partial(sort_kernel, slabs, width, part, len(ties)),
        out_shape=[jax.ShapeDtypeStruct((2 * rows, width), jnp.bfloat16)] * (slabs // 2),
        grid_spec=pltpu.PrefetchScalarGridSpec(
            num_scalar_prefetch=1,
            grid=(1,),
            in_specs=[pl.BlockSpec(order.shape, lambda i, s: (0, 0, 0)), x_spec, x_spec] + [UNREAD] * len(ties),
            out_specs=[out] * (slabs // 2),
        ),
        compiler_params=params(width),
        cost_estimate=cost(3.0),
        name="sort_columns",
    )(me, order, *[far(by_slab(x, slabs, width)) for x in xs], *ties)


def swap(x, slabs, offset):
    return lax.ppermute(x, "slab", [(i, i ^ offset) for i in range(slabs)])


def exchange(pieces):
    return [pieces[0]] + [swap(pieces[i], 2 * len(pieces), 2 * i) for i in range(1, len(pieces))]


def volume_kernel(slabs, window, messages, first, ties, idx_ref, *refs):
    refs = refs[ties:]
    piece_refs, refs = refs[: slabs // 2], refs[slabs // 2 :]
    if first:
        sums_ref, meta_ref, code_refs = refs[0], refs[1], refs[2:-4]
    else:
        meta_ref, sums_ref, code_refs = refs[0], refs[1], refs[2:-4]
    all_ref, line_ref, scalar_ref, sem = refs[-4:]
    width = sums_ref.shape[3]
    rows = all_ref.shape[1]
    pick = (iota((16, LANES), 0) == iota((16, LANES), 1)).astype(jnp.bfloat16)
    for offset in range(slabs):
        if first:
            for i in range(rows // width):
                at = 2 * rows + 16 * (offset % 2 * (rows // width) + i)
                meta_ref[offset, :, i * width : (i + 1) * width] = piece_refs[offset // 2][at : at + 16, :]
        meta = meta_ref[offset]
        all_ref[offset] = lax.dot_general(
            meta, pick, (((0,), (0,)), ((), ())), preferred_element_type=jnp.float32
        ).astype(jnp.bfloat16)
        line_ref[offset : offset + 1, :] = meta.astype(jnp.float32)[10:11, 0:LANES].astype(jnp.int32) * ALIGN
    copy = pltpu.make_async_copy(line_ref, scalar_ref, sem)
    copy.start()
    copy.wait()

    def slab_sums(slab):
        about, here = [], []
        for offset in range(slabs):
            start = pl.multiple_of(scalar_ref[offset, slab], ALIGN)
            about.append(all_ref[offset, pl.ds(start, window), :])
            start = pl.multiple_of(offset % 2 * rows + start, ALIGN)
            here.append(piece_refs[offset // 2][pl.ds(start, window), :])
        about, here = jnp.concatenate(about, axis=0), jnp.concatenate(here, axis=0)
        meta = lax.dot_general(pick, about, (((1,), (1,)), ((), ())), preferred_element_type=jnp.float32)
        weights = meta[0:8]
        own = meta[8:9] == jnp.asarray(slab, jnp.float32)
        block = jnp.broadcast_to(jnp.where(own, meta[9:10], -1.0), weights.shape)
        spread = jnp.concatenate([jnp.where(block == float(b), weights, 0.0) for b in range(NBLK)], axis=0)
        sums = jnp.dot(spread.astype(jnp.bfloat16), here, preferred_element_type=jnp.float32)
        sums_ref[:, slab] = sums.reshape(YWIN, KZ_DEV, width)

    if slabs <= 8:
        for slab in range(slabs):
            slab_sums(slab)
    else:
        lax.fori_loop(0, slabs, lambda slab, carry: (slab_sums(slab), carry)[1], 0)
    portion = code_refs[0].shape[1] - ALIGN
    lines = portion // (slabs * KZ_DEV)
    at = 0
    for code_ref, count in zip(code_refs, messages):
        for i in range(count):
            x = sums_ref[pl.ds(idx_ref[at] * lines, lines)].reshape(portion, width)
            code_ref[i, :portion, :], code_ref[i, portion:, :] = encode(x)
            at += 1


def volume_sums(window, index, messages, groups, pieces, meta, ties):
    slabs = 2 * len(pieces)
    width = pieces[0].shape[1]
    first = meta is None
    rows = pieces[0].shape[0] // 2
    if first:
        rows = rows * width // (width + 16)
    portion = YWIN // groups * slabs * KZ_DEV
    out_shape = [
        jax.ShapeDtypeStruct((YWIN, slabs, KZ_DEV, width), jnp.float32),
    ]
    if first:
        out_shape.append(jax.ShapeDtypeStruct((slabs, 16, rows), jnp.bfloat16))
    out_shape += [jax.ShapeDtypeStruct((count, portion + ALIGN, width), jnp.int16) for count in messages]
    done = pl.pallas_call(
        functools.partial(volume_kernel, slabs, window, messages, first, len(ties)),
        out_shape=out_shape,
        in_specs=[SCALARS] + [UNREAD] * len(ties) + [WHOLE] * (len(pieces) + (0 if first else 1)),
        out_specs=[WHOLE] * len(out_shape),
        scratch_shapes=[
            pltpu.VMEM((slabs, rows, LANES), jnp.bfloat16),
            pltpu.VMEM((slabs, LANES), jnp.int32),
            pltpu.SMEM((slabs, LANES), jnp.int32),
            pltpu.SemaphoreType.DMA,
        ],
        compiler_params=params(width),
        cost_estimate=cost(7.0),
        name="volume_sums",
    )(index, *ties, *[far(x) for x in pieces], *([] if first else [meta]))
    sums = done[0].reshape(groups, portion, width)
    return (sums, done[2:], done[1]) if first else (sums, done[1:], meta)


def encode(x):
    rows, width = x.shape
    groups = rows // 8
    tiles = x.reshape(groups, 8, width)
    size = jnp.abs(tiles)
    most = jnp.max(jnp.max(size, axis=1), axis=1, keepdims=True)
    level = jnp.ceil(jnp.log2(jnp.maximum(most, 1e-36)) * STEPS) + 1.0
    inverse = jnp.broadcast_to(jnp.exp2(level * (-1.0 / STEPS)), (groups, width)).reshape(groups, 1, width)
    share = jnp.maximum(size * inverse, 1e-12)
    root = jnp.minimum(share * lax.rsqrt(share) * TOP + 0.5, TOP)
    code = jnp.where(tiles < 0, -root, root).reshape(rows, width).astype(jnp.int32).astype(jnp.int16)
    eye = iota((width, width), 0) == iota((width, width), 1)
    lines = [
        jnp.sum(jnp.where(eye, level[i * width : (i + 1) * width], 0.0), axis=0, keepdims=True)
        for i in range(groups // width)
    ]
    lines.append(jnp.zeros((ALIGN - len(lines), width), jnp.float32))
    return code, jnp.concatenate(lines, axis=0).astype(jnp.int32).astype(jnp.int16)


def decode(code, lines):
    rows, width = code.shape
    groups = rows // 8
    x = code.astype(jnp.int32).astype(jnp.float32)
    lines = lines.astype(jnp.int32).astype(jnp.float32)
    eye = iota((width, width), 0) == iota((width, width), 1)
    level = jnp.concatenate(
        [jnp.sum(jnp.where(eye, lines[i : i + 1], 0.0), axis=1, keepdims=True) for i in range(groups // width)],
        axis=0,
    )
    scale = jnp.exp2(level * (1.0 / STEPS))
    scale = jnp.broadcast_to(scale, (groups, width)).reshape(groups, 1, width)
    share = x * jnp.abs(x) * (1.0 / (TOP * TOP))
    return (share.reshape(groups, 8, width) * scale).reshape(rows, width)


def hop_kernel(places, idx_ref, sums_ref, prev_ref, *refs):
    out_ref = refs[-1]
    rows = sums_ref.shape[1]
    for i, place in enumerate(places):
        x = sums_ref[idx_ref[i]] + decode(prev_ref[place, :rows, :], prev_ref[place, rows:, :])
        out_ref[i, :rows, :], out_ref[i, rows:, :] = encode(x)


def hop(index, sums, prev, places, ties):
    _, rows, width = sums.shape
    count = len(places)
    return pl.pallas_call(
        functools.partial(hop_kernel, places),
        out_shape=jax.ShapeDtypeStruct((count, rows + ALIGN, width), jnp.int16),
        in_specs=[SCALARS, WHOLE, WHOLE] + [UNREAD] * len(ties),
        out_specs=WHOLE,
        compiler_params=params(width),
        cost_estimate=cost(2.0 + count),
        name="hop",
    )(index, sums, prev, *ties)


def portions(z, groups, r):
    return jnp.where(z >= groups // 2, groups - 1 - r, r).astype(jnp.int32)


class AlongZ:
    def __init__(self, sums, first, payloads, z, groups):
        self.sums, self.z, self.groups, self.ends = sums, z, groups, []
        half = groups // 2
        got = [{r: self.send(x, [(0, 1)]) for r, x in zip(first, payloads)}]
        hops = []
        for k in range(2, half):
            got.append({})
            for r in range(groups - 1, k, -1):
                hops.append(functools.partial(self.move, got[k - 2], r, got[k - 1], r, [(k - 1, k)]))
        across = {}
        for r in range(groups - 1, half - 1, -1):
            hops.append(functools.partial(self.move, got[half - 2], r, across, groups - 1 - r, [(half - 1, half)]))
        outward = across
        for j in range(half - 1, 1, -1):
            kept, new = {}, {}
            hops.append(functools.partial(self.move, got[j - 2], j, kept, j, [(j - 1, j)], True))
            for r in range(j):
                hops.append(functools.partial(self.move, outward, r, new, r, [(j, j - 1)], r == j - 1))
            outward = new
        hops.append(functools.partial(self.move, outward, 0, {}, 0, [(1, 0), (0, 1)], True, True))
        self.hops, self.keep = hops, half - 1

    def send(self, payload, pairs):
        last = self.groups - 1
        return lax.ppermute(payload, "grp", pairs + [(last - a, last - b) for a, b in pairs])

    def move(self, source, r, target, place, pairs, final=False, both=False, ties=()):
        last = self.groups - 1
        wanted = jnp.full((1,), r, jnp.int32)
        if both:
            wanted = jnp.where(jnp.minimum(self.z, last - self.z) == 0, 1, 0).astype(jnp.int32).reshape(1)
        payload = hop(portions(self.z, self.groups, wanted), self.sums, source[r], [0], ties)
        target[place] = self.send(payload, pairs)
        if final or (len(pairs) == 1 and pairs[0] == (self.keep, self.keep + 1) and place == self.keep):
            self.ends.append((target[place], 0))
        return payload


def image_kernel(parts, zs, own_ref, *refs):
    tau_ref, high_ref, low_ref, out_ref = refs[-4:]
    each = len(refs[:-4]) // 3
    volume = []
    for c in range(3):
        sums_ref, coded = refs[c * each], refs[c * each + 1 : (c + 1) * each]
        rows = sums_ref.shape[1]
        x = sums_ref[0]
        for ref in coded:
            x = x + decode(ref[0, :rows, :], ref[0, rows:, :])
        volume.append(x)
    below = volume[2] + tau_ref[...]
    columns = []
    for c in range(2):
        x = volume[c] / below
        columns += [x[k * zs : (k + 1) * zs] for k in range(parts)]
    x = jnp.concatenate(columns, axis=1)
    x_high = x.astype(jnp.bfloat16)
    x_low = (x - x_high.astype(jnp.float32)).astype(jnp.bfloat16)
    dot = functools.partial(jnp.dot, preferred_element_type=jnp.float32)
    y = dot(high_ref[...], x_high) + (dot(high_ref[...], x_low) + dot(low_ref[...], x_high))
    span = x.shape[1] // 2
    width = span // parts
    real = y[:zs, :span] - y[zs:, span:]
    imag = y[zs:, :span] + y[:zs, span:]
    for k in range(parts):
        out_ref[0, k] = real[:, k * width : (k + 1) * width]
        out_ref[1, k] = imag[:, k * width : (k + 1) * width]


def image_of(own, fields, tau, zs):
    rows, width = fields[0][0].shape[1:]
    parts = rows // zs
    operands, specs = [], []
    for sums, ends in fields:
        operands.append(sums)
        specs.append(pl.BlockSpec((1, rows, width), lambda i, s: (s[0], 0, 0)))
        for payload, place in ends:
            operands.append(payload)
            specs.append(pl.BlockSpec((1, rows + ALIGN, width), functools.partial(lambda place, i, s: (place, 0, 0), place)))
    steps = np.arange(zs)
    angles = (steps[:, None] * steps[None, :] % zs) * (2.0 * math.pi / zs)
    table = (np.concatenate([np.cos(angles), np.sin(angles)], axis=0) / math.sqrt(zs)).astype(np.float32)
    high = table.astype(jnp.bfloat16)
    low = (table - high.astype(np.float32)).astype(jnp.bfloat16)
    for x in (tau.reshape(1, width), jnp.asarray(high), jnp.asarray(low)):
        operands.append(x)
        specs.append(pl.BlockSpec(x.shape, lambda i, s: (0, 0)))
    return pl.pallas_call(
        functools.partial(image_kernel, parts, zs),
        out_shape=jax.ShapeDtypeStruct((2, parts, zs, width), jnp.float32),
        grid_spec=pltpu.PrefetchScalarGridSpec(
            num_scalar_prefetch=1,
            grid=(1,),
            in_specs=specs,
            out_specs=pl.BlockSpec((2, parts, zs, width), lambda i, s: (0, 0, 0, 0)),
        ),
        compiler_params=params(width),
        cost_estimate=cost(6.0),
        name="image_of",
    )(own, *[far(x) for x in operands])


def on_device(spectra, ctf_sq, dest, block, pattern, pattern_table, tau):
    slabs, groups = lax.axis_size("slab"), lax.axis_size("grp")
    rows, kx = ctf_sq.shape
    capacity = max(2, 2 * rows // slabs)
    window = min(rows, -(-capacity // ALIGN) * ALIGN + ALIGN)
    width = kx // slabs
    slab, z = lax.axis_index("slab"), lax.axis_index("grp")
    me = slab.astype(jnp.int32).reshape(1)
    ids = jnp.stack([dest[:, 0], block, pattern])
    ids, ctf_sq, spectra = [(x, swap(x, slabs, 1)) for x in (ids, ctf_sq, spectra)]
    order, ctf = plan_rows(slabs, window, me, ids, pattern_table, ctf_sq)
    first = list(range(groups - 1, 1, -1))
    index = portions(z, groups, np.array(first))

    def volume(piece, meta, ties):
        sums, payloads, meta = volume_sums(window, index, [1] * len(first), groups, piece, meta, ties)
        return AlongZ(sums, first, payloads, z, groups), payloads[0], meta

    real = sort_columns(slabs, me, order, spectra, 0, ())
    ctf, real_there = exchange(ctf), exchange(real)
    imag = sort_columns(slabs, me, order, spectra, 1, (real[0],))
    ctf_part, coded, meta = volume(ctf, None, (imag[0],))
    imag_there = exchange(imag)
    real_part, coded, _ = volume(real_there, meta, (coded,))
    tie = coded
    early = len(ctf_part.hops) - 1
    for step in ctf_part.hops[:early]:
        tie = step(ties=(tie,))
    imag_part, coded, _ = volume(imag_there, meta, (tie,))
    left = imag_part.hops[1:]
    if groups == 4:
        left = left[::-1]
    steps = real_part.hops[:-1] + imag_part.hops[:1] + ctf_part.hops[early:] + real_part.hops[-1:] + left
    tie = coded
    for step in steps:
        tie = step(ties=(tie,))
    fields = [(part.sums, part.ends) for part in (ctf_part, real_part, imag_part)]
    tau_here = lax.dynamic_slice_in_dim(tau, slab * width, width, 0)
    own = z.astype(jnp.int32).reshape(1)
    return image_of(own, [fields[1], fields[2], fields[0]], tau_here, KZ_DEV * slabs)


def solution(mesh):
    in_specs = (
        P(("grp", "slab"), None),
        P(("grp", "slab"), None),
        P(("grp", "slab"), None),
        P(("grp", "slab")),
        P(("grp", "slab")),
        P(),
        P(),
    )
    out_specs = P(None, "grp", None, "slab")
    return jax.shard_map(
        on_device, mesh=mesh, in_specs=in_specs, out_specs=out_specs, check_vma=False
    )
```

```python
import functools
import math

import jax
import jax.numpy as jnp
import numpy as np
from jax import lax
from jax.experimental import pallas as pl
from jax.experimental.pallas import tpu as pltpu
from jax.sharding import PartitionSpec as P

KZ_DEV = 32
YWIN = 16
NBLK = 64
LANES = 128
ALIGN = 16
TOP = 32767.0
STEPS = 256.0
VMEM = 60 * 1024 * 1024

WHOLE = pl.BlockSpec(memory_space=pltpu.VMEM)
SCALARS = pl.BlockSpec(memory_space=pltpu.SMEM)
UNREAD = pl.BlockSpec(memory_space=pl.ANY)


def params(width):
    return pltpu.CompilerParams(vmem_limit_bytes=VMEM if width < LANES else VMEM // 2)


def far(x):
    return pltpu.with_memory_space_constraint(x, pltpu.HBM)


def cost(micros):
    return pl.CostEstimate(flops=0, bytes_accessed=int(micros * 3.0e6), transcendentals=0)


def iota(shape, axis):
    return lax.broadcasted_iota(jnp.int32, shape, axis)


def plan(slabs, window, dest, block, pattern, table):
    rows = dest.shape[1]
    mine = (dest == iota((slabs, rows), 0)).astype(jnp.float32)
    before = (iota((rows, rows), 0) < iota((rows, rows), 1)).astype(jnp.bfloat16)
    rank = jnp.dot(mine.astype(jnp.bfloat16), before, preferred_element_type=jnp.float32)
    counts = jnp.sum(mine, axis=1, keepdims=True)
    slab_of = iota((slabs, rows), 0)
    first = jnp.sum(jnp.where(slab_of < dest, counts, 0.0), axis=0, keepdims=True)
    target = (first + jnp.sum(mine * rank, axis=0, keepdims=True)).astype(jnp.int32)
    order = (target == iota((rows, rows), 0)).astype(jnp.bfloat16)
    ids = (pattern == iota((table.shape[1], rows), 0)).astype(jnp.bfloat16)
    weights = jnp.dot(table, ids, preferred_element_type=jnp.float32)
    line = iota((8, rows), 0)
    named = jnp.where(line == 0, dest, jnp.where(line == 1, block, 0)).astype(jnp.float32)
    given = jnp.concatenate([weights, named], axis=0).astype(jnp.bfloat16)
    ordered = lax.dot_general(given, order, (((1,), (1,)), ((), ())), preferred_element_type=jnp.float32)
    start = jnp.sum(jnp.where(slab_of < iota((slabs, rows), 1), counts, 0.0), axis=0, keepdims=True)
    start = jnp.minimum(start.astype(jnp.int32) // ALIGN, (rows - window) // ALIGN).astype(jnp.float32)
    meta = jnp.where(iota((16, rows), 0) == 10, start, ordered).astype(jnp.bfloat16)
    return order, meta


def piece_of(x_ref, column, width):
    if len(x_ref.shape) == 3:
        return x_ref[column]
    return x_ref[:, pl.ds(pl.multiple_of(column * width, width), width)]


def by_slab(x, slabs, width):
    if width % LANES == 0:
        return x
    return x.reshape(x.shape[0], -1, width).transpose(1, 0, 2)


def sorted_piece(order, x_ref, column, width):
    piece = piece_of(x_ref, column, width)
    return jnp.dot(order, piece, preferred_element_type=jnp.float32).astype(jnp.bfloat16)


def plan_kernel(slabs, window, width, me_ref, *refs):
    ids_refs, table_ref, x_refs, order_ref, out_refs = refs[0:2], refs[2], refs[3:5], refs[5], refs[6:]
    rows = order_ref.shape[1]
    lines = 16 * (rows // width)
    for half in range(2):
        ids = ids_refs[half][...]
        order, meta = plan(slabs, window, ids[0:1], ids[1:2], ids[2:3], table_ref[...])
        order_ref[half] = order
        for i, out in enumerate(out_refs):
            column = jnp.bitwise_xor(me_ref[0], 2 * i)
            out[half * rows : (half + 1) * rows, :] = sorted_piece(order, x_refs[half], column, width)
            for j in range(rows // width):
                at = 2 * rows + half * lines + 16 * j
                out[at : at + 16, :] = meta[:, j * width : (j + 1) * width]


def plan_rows(slabs, window, me, ids, table, xs):
    rows, kx = xs[0].shape
    width = kx // slabs
    out = jax.ShapeDtypeStruct((2 * rows + 32 * (rows // width), width), jnp.bfloat16)
    done = pl.pallas_call(
        functools.partial(plan_kernel, slabs, window, width),
        out_shape=[jax.ShapeDtypeStruct((2, rows, rows), jnp.bfloat16)] + [out] * (slabs // 2),
        in_specs=[SCALARS] + [WHOLE] * 5,
        out_specs=[WHOLE] * (1 + slabs // 2),
        compiler_params=params(width),
        cost_estimate=cost(6.0),
        name="plan_rows",
    )(me, far(ids[0]), ids[1], far(table.T), far(by_slab(xs[0], slabs, width)), by_slab(xs[1], slabs, width))
    return done[0], done[1:]


def sort_kernel(slabs, width, part, ties, me_ref, order_ref, *refs):
    x_refs, out_refs = refs[0:2], refs[2 + ties :]
    rows = order_ref.shape[1]
    for i, out in enumerate(out_refs):
        column = jnp.bitwise_xor(me_ref[0], 2 * i) + part * slabs
        for half in range(2):
            out[half * rows : (half + 1) * rows, :] = sorted_piece(order_ref[half], x_refs[half], column, width)


def sort_columns(slabs, me, order, xs, part, ties):
    rows, kx = order.shape[1], xs[0].shape[1] // 2
    width = kx // slabs
    if width % LANES == 0:
        x_spec = pl.BlockSpec((rows, kx), functools.partial(lambda part, i, s: (0, part), part))
        part = 0
    else:
        x_spec = pl.BlockSpec((2 * slabs, rows, width), lambda i, s: (0, 0, 0))
    out = pl.BlockSpec((2 * rows, width), lambda i, s: (0, 0))
    return pl.pallas_call(
        functools.partial(sort_kernel, slabs, width, part, len(ties)),
        out_shape=[jax.ShapeDtypeStruct((2 * rows, width), jnp.bfloat16)] * (slabs // 2),
        grid_spec=pltpu.PrefetchScalarGridSpec(
            num_scalar_prefetch=1,
            grid=(1,),
            in_specs=[pl.BlockSpec(order.shape, lambda i, s: (0, 0, 0)), x_spec, x_spec] + [UNREAD] * len(ties),
            out_specs=[out] * (slabs // 2),
        ),
        compiler_params=params(width),
        cost_estimate=cost(3.0),
        name="sort_columns",
    )(me, order, *[far(by_slab(x, slabs, width)) for x in xs], *ties)


def swap(x, slabs, offset):
    return lax.ppermute(x, "slab", [(i, i ^ offset) for i in range(slabs)])


def exchange(pieces):
    return [pieces[0]] + [swap(pieces[i], 2 * len(pieces), 2 * i) for i in range(1, len(pieces))]


def volume_kernel(slabs, window, messages, first, ties, idx_ref, *refs):
    refs = refs[ties:]
    piece_refs, refs = refs[: slabs // 2], refs[slabs // 2 :]
    if first:
        sums_ref, meta_ref, code_refs = refs[0], refs[1], refs[2:-4]
    else:
        meta_ref, sums_ref, code_refs = refs[0], refs[1], refs[2:-4]
    all_ref, line_ref, scalar_ref, sem = refs[-4:]
    width = sums_ref.shape[3]
    rows = all_ref.shape[1]
    pick = (iota((16, LANES), 0) == iota((16, LANES), 1)).astype(jnp.bfloat16)
    for offset in range(slabs):
        if first:
            for i in range(rows // width):
                at = 2 * rows + 16 * (offset % 2 * (rows // width) + i)
                meta_ref[offset, :, i * width : (i + 1) * width] = piece_refs[offset // 2][at : at + 16, :]
        meta = meta_ref[offset]
        all_ref[offset] = lax.dot_general(
            meta, pick, (((0,), (0,)), ((), ())), preferred_element_type=jnp.float32
        ).astype(jnp.bfloat16)
        line_ref[offset : offset + 1, :] = meta.astype(jnp.float32)[10:11, 0:LANES].astype(jnp.int32) * ALIGN
    copy = pltpu.make_async_copy(line_ref, scalar_ref, sem)
    copy.start()
    copy.wait()

    def slab_sums(slab):
        about, here = [], []
        for offset in range(slabs):
            start = pl.multiple_of(scalar_ref[offset, slab], ALIGN)
            about.append(all_ref[offset, pl.ds(start, window), :])
            start = pl.multiple_of(offset % 2 * rows + start, ALIGN)
            here.append(piece_refs[offset // 2][pl.ds(start, window), :])
        about, here = jnp.concatenate(about, axis=0), jnp.concatenate(here, axis=0)
        meta = lax.dot_general(pick, about, (((1,), (1,)), ((), ())), preferred_element_type=jnp.float32)
        weights = meta[0:8]
        own = meta[8:9] == jnp.asarray(slab, jnp.float32)
        block = jnp.broadcast_to(jnp.where(own, meta[9:10], -1.0), weights.shape)
        spread = jnp.concatenate([jnp.where(block == float(b), weights, 0.0) for b in range(NBLK)], axis=0)
        sums = jnp.dot(spread.astype(jnp.bfloat16), here, preferred_element_type=jnp.float32)
        sums_ref[:, slab] = sums.reshape(YWIN, KZ_DEV, width)

    if slabs <= 8:
        for slab in range(slabs):
            slab_sums(slab)
    else:
        lax.fori_loop(0, slabs, lambda slab, carry: (slab_sums(slab), carry)[1], 0)
    portion = code_refs[0].shape[1] - ALIGN
    lines = portion // (slabs * KZ_DEV)
    at = 0
    for code_ref, count in zip(code_refs, messages):
        for i in range(count):
            x = sums_ref[pl.ds(idx_ref[at] * lines, lines)].reshape(portion, width)
            code_ref[i, :portion, :], code_ref[i, portion:, :] = encode(x)
            at += 1


def volume_sums(window, index, messages, groups, pieces, meta, ties):
    slabs = 2 * len(pieces)
    width = pieces[0].shape[1]
    first = meta is None
    rows = pieces[0].shape[0] // 2
    if first:
        rows = rows * width // (width + 16)
    portion = YWIN // groups * slabs * KZ_DEV
    out_shape = [
        jax.ShapeDtypeStruct((YWIN, slabs, KZ_DEV, width), jnp.float32),
    ]
    if first:
        out_shape.append(jax.ShapeDtypeStruct((slabs, 16, rows), jnp.bfloat16))
    out_shape += [jax.ShapeDtypeStruct((count, portion + ALIGN, width), jnp.int16) for count in messages]
    done = pl.pallas_call(
        functools.partial(volume_kernel, slabs, window, messages, first, len(ties)),
        out_shape=out_shape,
        in_specs=[SCALARS] + [UNREAD] * len(ties) + [WHOLE] * (len(pieces) + (0 if first else 1)),
        out_specs=[WHOLE] * len(out_shape),
        scratch_shapes=[
            pltpu.VMEM((slabs, rows, LANES), jnp.bfloat16),
            pltpu.VMEM((slabs, LANES), jnp.int32),
            pltpu.SMEM((slabs, LANES), jnp.int32),
            pltpu.SemaphoreType.DMA,
        ],
        compiler_params=params(width),
        cost_estimate=cost(7.0),
        name="volume_sums",
    )(index, *ties, *([far(x) for x in pieces] if meta is None else pieces), *([] if first else [meta]))
    sums = done[0].reshape(groups, portion, width)
    return (sums, done[2:], done[1]) if first else (sums, done[1:], meta)


def encode(x):
    rows, width = x.shape
    groups = rows // 8
    tiles = x.reshape(groups, 8, width)
    size = jnp.abs(tiles)
    most = jnp.max(jnp.max(size, axis=1), axis=1, keepdims=True)
    level = jnp.ceil(jnp.log2(jnp.maximum(most, 1e-36)) * STEPS) + 1.0
    inverse = jnp.broadcast_to(jnp.exp2(level * (-1.0 / STEPS)), (groups, width)).reshape(groups, 1, width)
    share = jnp.maximum(size * inverse, 1e-12)
    root = jnp.minimum(share * lax.rsqrt(share) * TOP + 0.5, TOP)
    code = jnp.where(tiles < 0, -root, root).reshape(rows, width).astype(jnp.int32).astype(jnp.int16)
    eye = iota((width, width), 0) == iota((width, width), 1)
    lines = [
        jnp.sum(jnp.where(eye, level[i * width : (i + 1) * width], 0.0), axis=0, keepdims=True)
        for i in range(groups // width)
    ]
    lines.append(jnp.zeros((ALIGN - len(lines), width), jnp.float32))
    return code, jnp.concatenate(lines, axis=0).astype(jnp.int32).astype(jnp.int16)


def decode(code, lines):
    rows, width = code.shape
    groups = rows // 8
    x = code.astype(jnp.int32).astype(jnp.float32)
    lines = lines.astype(jnp.int32).astype(jnp.float32)
    eye = iota((width, width), 0) == iota((width, width), 1)
    level = jnp.concatenate(
        [jnp.sum(jnp.where(eye, lines[i : i + 1], 0.0), axis=1, keepdims=True) for i in range(groups // width)],
        axis=0,
    )
    scale = jnp.exp2(level * (1.0 / STEPS))
    scale = jnp.broadcast_to(scale, (groups, width)).reshape(groups, 1, width)
    share = x * jnp.abs(x) * (1.0 / (TOP * TOP))
    return (share.reshape(groups, 8, width) * scale).reshape(rows, width)


def hop_kernel(places, idx_ref, sums_ref, prev_ref, *refs):
    out_ref = refs[-1]
    rows = sums_ref.shape[1]
    for i, place in enumerate(places):
        x = sums_ref[idx_ref[i]] + decode(prev_ref[place, :rows, :], prev_ref[place, rows:, :])
        out_ref[i, :rows, :], out_ref[i, rows:, :] = encode(x)


def hop(index, sums, prev, places, ties):
    _, rows, width = sums.shape
    count = len(places)
    return pl.pallas_call(
        functools.partial(hop_kernel, places),
        out_shape=jax.ShapeDtypeStruct((count, rows + ALIGN, width), jnp.int16),
        in_specs=[SCALARS, WHOLE, WHOLE] + [UNREAD] * len(ties),
        out_specs=WHOLE,
        compiler_params=params(width),
        cost_estimate=cost(2.0 + count),
        name="hop",
    )(index, sums, prev, *ties)


def portions(z, groups, r):
    return jnp.where(z >= groups // 2, groups - 1 - r, r).astype(jnp.int32)


class AlongZ:
    def __init__(self, sums, first, payloads, z, groups):
        self.sums, self.z, self.groups, self.ends = sums, z, groups, []
        half = groups // 2
        got = [{r: self.send(x, [(0, 1)]) for r, x in zip(first, payloads)}]
        hops = []
        for k in range(2, half):
            got.append({})
            for r in range(groups - 1, k, -1):
                hops.append(functools.partial(self.move, got[k - 2], r, got[k - 1], r, [(k - 1, k)]))
        across = {}
        for r in range(groups - 1, half - 1, -1):
            hops.append(functools.partial(self.move, got[half - 2], r, across, groups - 1 - r, [(half - 1, half)]))
        outward = across
        for j in range(half - 1, 1, -1):
            kept, new = {}, {}
            hops.append(functools.partial(self.move, got[j - 2], j, kept, j, [(j - 1, j)], True))
            for r in range(j):
                hops.append(functools.partial(self.move, outward, r, new, r, [(j, j - 1)], r == j - 1))
            outward = new
        hops.append(functools.partial(self.move, outward, 0, {}, 0, [(1, 0), (0, 1)], True, True))
        self.hops, self.keep = hops, half - 1

    def send(self, payload, pairs):
        last = self.groups - 1
        return lax.ppermute(payload, "grp", pairs + [(last - a, last - b) for a, b in pairs])

    def move(self, source, r, target, place, pairs, final=False, both=False, ties=()):
        last = self.groups - 1
        wanted = jnp.full((1,), r, jnp.int32)
        if both:
            wanted = jnp.where(jnp.minimum(self.z, last - self.z) == 0, 1, 0).astype(jnp.int32).reshape(1)
        payload = hop(portions(self.z, self.groups, wanted), self.sums, source[r], [0], ties)
        target[place] = self.send(payload, pairs)
        if final or (len(pairs) == 1 and pairs[0] == (self.keep, self.keep + 1) and place == self.keep):
            self.ends.append((target[place], 0))
        return payload


def image_kernel(parts, zs, own_ref, *refs):
    tau_ref, high_ref, low_ref, out_ref = refs[-4:]
    each = len(refs[:-4]) // 3
    volume = []
    for c in range(3):
        sums_ref, coded = refs[c * each], refs[c * each + 1 : (c + 1) * each]
        rows = sums_ref.shape[1]
        x = sums_ref[0]
        for ref in coded:
            x = x + decode(ref[0, :rows, :], ref[0, rows:, :])
        volume.append(x)
    below = volume[2] + tau_ref[...]
    columns = []
    for c in range(2):
        x = volume[c] / below
        columns += [x[k * zs : (k + 1) * zs] for k in range(parts)]
    x = jnp.concatenate(columns, axis=1)
    x_high = x.astype(jnp.bfloat16)
    x_low = (x - x_high.astype(jnp.float32)).astype(jnp.bfloat16)
    dot = functools.partial(jnp.dot, preferred_element_type=jnp.float32)
    y = dot(high_ref[...], x_high) + (dot(high_ref[...], x_low) + dot(low_ref[...], x_high))
    span = x.shape[1] // 2
    width = span // parts
    real = y[:zs, :span] - y[zs:, span:]
    imag = y[zs:, :span] + y[:zs, span:]
    for k in range(parts):
        out_ref[0, k] = real[:, k * width : (k + 1) * width]
        out_ref[1, k] = imag[:, k * width : (k + 1) * width]


def image_of(own, fields, tau, zs):
    rows, width = fields[0][0].shape[1:]
    parts = rows // zs
    operands, specs = [], []
    for sums, ends in fields:
        operands.append(sums)
        specs.append(pl.BlockSpec((1, rows, width), lambda i, s: (s[0], 0, 0)))
        for payload, place in ends:
            operands.append(payload)
            specs.append(pl.BlockSpec((1, rows + ALIGN, width), functools.partial(lambda place, i, s: (place, 0, 0), place)))
    late = [payload for payload, _ in fields[1][1]]
    steps = np.arange(zs)
    angles = (steps[:, None] * steps[None, :] % zs) * (2.0 * math.pi / zs)
    table = (np.concatenate([np.cos(angles), np.sin(angles)], axis=0) / math.sqrt(zs)).astype(np.float32)
    high = table.astype(jnp.bfloat16)
    low = (table - high.astype(np.float32)).astype(jnp.bfloat16)
    for x in (tau.reshape(1, width), jnp.asarray(high), jnp.asarray(low)):
        operands.append(x)
        specs.append(pl.BlockSpec(x.shape, lambda i, s: (0, 0)))
    return pl.pallas_call(
        functools.partial(image_kernel, parts, zs),
        out_shape=jax.ShapeDtypeStruct((2, parts, zs, width), jnp.float32),
        grid_spec=pltpu.PrefetchScalarGridSpec(
            num_scalar_prefetch=1,
            grid=(1,),
            in_specs=specs,
            out_specs=pl.BlockSpec((2, parts, zs, width), lambda i, s: (0, 0, 0, 0)),
        ),
        compiler_params=params(width),
        cost_estimate=cost(6.0),
        name="image_of",
    )(own, *[x if any(x is y for y in late) else far(x) for x in operands])


def on_device(spectra, ctf_sq, dest, block, pattern, pattern_table, tau):
    slabs, groups = lax.axis_size("slab"), lax.axis_size("grp")
    rows, kx = ctf_sq.shape
    capacity = max(2, 2 * rows // slabs)
    window = min(rows, -(-capacity // ALIGN) * ALIGN + ALIGN)
    width = kx // slabs
    slab, z = lax.axis_index("slab"), lax.axis_index("grp")
    me = slab.astype(jnp.int32).reshape(1)
    ids = jnp.stack([dest[:, 0], block, pattern])
    ids, ctf_sq, spectra = [(x, swap(x, slabs, 1)) for x in (ids, ctf_sq, spectra)]
    order, ctf = plan_rows(slabs, window, me, ids, pattern_table, ctf_sq)
    first = list(range(groups - 1, 1, -1))
    index = portions(z, groups, np.array(first))

    def volume(piece, meta, ties):
        sums, payloads, meta = volume_sums(window, index, [1] * len(first), groups, piece, meta, ties)
        return AlongZ(sums, first, payloads, z, groups), payloads[0], meta

    real = sort_columns(slabs, me, order, spectra, 0, ())
    ctf, real_there = exchange(ctf), exchange(real)
    imag = sort_columns(slabs, me, order, spectra, 1, (real[0],))
    ctf_part, coded, meta = volume(ctf, None, (imag[0],))
    imag_there = exchange(imag)
    real_part, coded, _ = volume(real_there, meta, (coded,))
    tie = coded
    early = len(ctf_part.hops) - 1
    for step in ctf_part.hops[:early]:
        tie = step(ties=(tie,))
    imag_part, coded, _ = volume(imag_there, meta, (tie,))
    left = imag_part.hops[1:]
    if groups == 4:
        left = left[::-1]
    steps = real_part.hops[:-1] + imag_part.hops[:1] + ctf_part.hops[early:] + real_part.hops[-1:] + left
    tie = coded
    for step in steps:
        tie = step(ties=(tie,))
    fields = [(part.sums, part.ends) for part in (ctf_part, real_part, imag_part)]
    tau_here = lax.dynamic_slice_in_dim(tau, slab * width, width, 0)
    own = z.astype(jnp.int32).reshape(1)
    return image_of(own, [fields[1], fields[2], fields[0]], tau_here, KZ_DEV * slabs)


def solution(mesh):
    in_specs = (
        P(("grp", "slab"), None),
        P(("grp", "slab"), None),
        P(("grp", "slab"), None),
        P(("grp", "slab")),
        P(("grp", "slab")),
        P(),
        P(),
    )
    out_specs = P(None, "grp", None, "slab")
    return jax.shard_map(
        on_device, mesh=mesh, in_specs=in_specs, out_specs=out_specs, check_vma=False
    )
```
